256 devices in a mesh: role: 2 (over x_hi), dp: 8 (over x_lo, y), seq: 16 (over z, core).
Axes of the slice: x: 4 (x_hi: 2, x_lo: 2; x = x_hi * 2 + x_lo), y: 4, z: 8, core: 2. Of those that a mesh axis runs over, the one named last changes fastest.
Arguments:
- latents: bfloat16 [2, 8, 2048, 64], P('role', 'dp', 'seq'), may hold values from -6 to 6
- next_latents: bfloat16 [8, 2048, 64], P('dp', 'seq'), may hold values from -6 to 6
- noise: bfloat16 [8, 2048, 64], P('dp', 'seq'), may hold values from -6 to 6
- advantage: float32 [8], P('dp'), may hold values from -3 to 3
- old_logp: float32 [8], P('dp'), may hold values from -2.6 to -1.2
- timesteps: int32 [2, 8], P('role', 'dp'), may hold values from 0 to 9
- embed_weight: bfloat16 [64, 3072], replicated, may hold values from -0.75 to 0.75
- modulation: float32 [10, 2, 3072], replicated, may hold values from -24 to 24
- qkv_weight: bfloat16 [2, 3, 3072, 4096], P('role', None, 'dp', 'seq'), may hold values from -7.2 to 7.2
- head_weight: bfloat16 [2, 4096, 64], P('role', 'seq'), may hold values from -3 to 3
Outputs:
- fresh_latents: bfloat16 [2, 8, 2048, 64], P('role', 'dp', 'seq')
- head_next: bfloat16 [2, 4096, 64], P('role', 'seq')
The draws below stay inside these ranges and needn't reach their ends.
All inputs are finite; a program needn't handle non-finite values.
Results may differ from the reference program's by a relative error of at most 0.012.
The reference program's roundings to bfloat16 on the way (of `embedded`, `modulated`, `probs`, `attended` and `weighted`) count: a program that leaves them out, or rounds other values in their place, can miss the bound.
Values may be sent and summed in bfloat16 or wider, within the bound.
No kernel may reach another device: no remote copies, remote signals or barrier semaphores. Data moves between devices by JAX's collectives and lax.ppermute only.
A program may use at most 128 MiB of HBM per device.

```python
import jax
import jax.numpy as jnp
from jax import lax

D = 3072
HEADS = 32
HD = 128
CHANNELS = 64
STEPS = 10
TOK_DEV = 128
INNER = 4096
SEQ_LEN = 2048
ROLL = 8


def draw_modulation(key, part):
    key = jax.random.fold_in(key, 11)
    standard = jnp.clip(jax.random.normal(key, (STEPS, 2, D), jnp.float32), -6.0, 6.0)
    result = 0.5 * standard
    return result


def draw_qkv_weight(key, part):
    key = jax.random.fold_in(key, 23)
    query_key, fresh_key, value_key, order_key, jitter_key = jax.random.split(key, 5)
    shape_one = (2, D, INNER)
    queries = 1.2 * jnp.clip(jax.random.normal(query_key, shape_one, jnp.float32), -6.0, 6.0)
    fresh_keys = 1.2 * jnp.clip(jax.random.normal(fresh_key, shape_one, jnp.float32), -6.0, 6.0)
    head_index = jnp.arange(INNER) // HD
    head_level = head_index.astype(jnp.float32) / max(HEADS - 1, 1)
    reversed_order = jax.random.bernoulli(order_key, 0.5)
    head_level = jnp.where(reversed_order, 1.0 - head_level, head_level)
    head_jitter = jax.random.uniform(jitter_key, (HEADS,), jnp.float32, 0.75, 1.0)
    value_scale = 0.25 ** head_level * head_jitter[head_index]
    values_part = 1.2 * value_scale * jnp.clip(jax.random.normal(value_key, shape_one, jnp.float32), -6.0, 6.0)
    keys_part = fresh_keys
    return jnp.stack([queries, keys_part, values_part], axis=1).astype(jnp.bfloat16)


def draw_latents(key, part):
    key = jax.random.fold_in(key, 37)
    low_key, high_key, flip_key, jitter_key, common_key, own_key = jax.random.split(key, 6)
    blocks = SEQ_LEN // TOK_DEV
    low = jax.random.uniform(low_key, (2, ROLL), jnp.float32, 0.1, 0.3)
    high = jax.random.uniform(high_key, (2, ROLL), jnp.float32, 0.75, 0.95)
    flipped = jax.random.bernoulli(flip_key, 0.5, (2, ROLL))
    position = (jnp.arange(SEQ_LEN) // TOK_DEV).astype(jnp.float32) / max(blocks - 1, 1)
    ramp = jnp.where(flipped[:, :, None], 1.0 - position[None, None, :], position[None, None, :])
    jitter = jnp.repeat(jax.random.uniform(jitter_key, (2, ROLL, blocks), jnp.float32, -0.03, 0.03), TOK_DEV, axis=2)
    mixing = jnp.clip(low[:, :, None] + (high - low)[:, :, None] * ramp + jitter, 0.05, 0.98)
    common = jnp.repeat(jax.random.normal(common_key, (2, ROLL, blocks, CHANNELS), jnp.float32), TOK_DEV, axis=2)
    own_part = jax.random.normal(own_key, (2, ROLL, SEQ_LEN, CHANNELS), jnp.float32)
    mixed = mixing[..., None] * common + jnp.sqrt(1.0 - mixing * mixing)[..., None] * own_part
    return jnp.clip(mixed, -6.0, 6.0).astype(jnp.bfloat16)


def draw_head_weight(key, part):
    key = jax.random.fold_in(key, 41)
    standard = jnp.clip(jax.random.normal(key, (2, INNER, CHANNELS), jnp.float32), -6.0, 6.0)
    spread = max(0.25, 4.0 / INNER ** 0.5)
    return (spread * standard).astype(jnp.bfloat16)


def set_ends(entries, stream_key, smallest, largest):
    longest = entries.shape.index(max(entries.shape))
    spots = []
    for shift in (0, 1):
        where = [jax.random.randint(jax.random.fold_in(stream_key, axis), (), 0, length) for axis, length in enumerate(entries.shape)]
        where[longest] = (where[longest] + shift) % entries.shape[longest]
        spots.append(tuple(where))
    return entries.at[spots[0]].set(smallest).at[spots[1]].set(largest)


def block_levels(stream_key, dims, pieces, least, high):
    def one(dim, blocks):
        heights = jax.random.uniform(jax.random.fold_in(jax.random.fold_in(stream_key, 6), dim), (blocks,), jnp.float32, least / len(pieces), high / len(pieces))
        return jnp.repeat(jnp.exp(heights), dims[dim] // blocks).reshape((-1,) + (1,) * (len(dims) - dim - 1))

    level = one(*pieces[0])
    for cut in pieces[1:]:
        level = level * one(*cut)
    return level


def gaussian(stream_key, shape, deviation, bound, pieces=(), kind=jnp.bfloat16):
    loudness = block_levels(stream_key, shape, pieces, -0.22, 0.18) if pieces else 1.0
    values = jax.random.normal(stream_key, shape, jnp.float32) * deviation * loudness
    return jnp.minimum(jnp.maximum(values, -bound), bound).astype(kind)


def setup_inputs(seed: int = 0) -> dict:
    keys = jax.random.split(jax.random.key(seed), 11)
    return {
        "latents": draw_latents(jax.random.fold_in(keys[10], 71), 0),
        "next_latents": gaussian(keys[1], (ROLL, SEQ_LEN, CHANNELS), 1.0, 6.0, ((0, 8), (1, 16))),
        "noise": gaussian(keys[2], (ROLL, SEQ_LEN, CHANNELS), 1.0, 6.0, ((0, 8), (1, 16))),
        "advantage": gaussian(keys[3], (ROLL,), 1.0, 3.0, ((0, 8),), jnp.float32),
        "old_logp": jnp.clip(-2.6 + 1.3999999 * jax.random.uniform(keys[4], (ROLL,), jnp.float32) ** block_levels(keys[4], (ROLL,), ((0, 8),), -0.2, 0.2), -2.6, -1.2),
        "timesteps": set_ends(jax.random.randint(keys[5], (2, ROLL), 0, STEPS), jax.random.fold_in(keys[5], 1), 0, STEPS - 1).astype(jnp.int32),
        "embed_weight": gaussian(keys[6], (CHANNELS, D), CHANNELS ** -0.5, 0.75),
        "modulation": draw_modulation(jax.random.fold_in(keys[10], 71), 0),
        "qkv_weight": draw_qkv_weight(jax.random.fold_in(keys[10], 71), 0),
        "head_weight": draw_head_weight(jax.random.fold_in(keys[10], 71), 0),
    }


noise_level = 0.8
step_size = 0.5
norm_eps = 1e-06
update_eps = 1e-06

def normalize(embedded, shift_scale):
    values = embedded.astype(jnp.float32)
    center = lax.optimization_barrier(jnp.mean(values, axis=-1, keepdims=True))
    spread = lax.optimization_barrier(jnp.mean((values - center) * (values - center), axis=-1, keepdims=True))
    normed = (values - center) * lax.rsqrt(spread + norm_eps)
    return (normed * (1.0 + shift_scale[1]) + shift_scale[0]).astype(jnp.bfloat16)

def forward(latent, step_index, qkv_copy, head_copy, embed_weight, modulation):
    embedded = jnp.dot(latent, embed_weight, preferred_element_type=jnp.float32).astype(jnp.bfloat16)
    shift_scale = lax.dynamic_index_in_dim(modulation, step_index, 0, keepdims=False)
    modulated = normalize(embedded, shift_scale)
    factor = 1.0 / D ** 0.5
    queries = (jnp.dot(modulated, qkv_copy[0], preferred_element_type=jnp.float32) * factor).astype(jnp.bfloat16)
    keys_all = (jnp.dot(modulated, qkv_copy[1], preferred_element_type=jnp.float32) * factor).astype(jnp.bfloat16)
    values_all = (jnp.dot(modulated, qkv_copy[2], preferred_element_type=jnp.float32) * factor).astype(jnp.bfloat16)
    length = latent.shape[0]

    def split_heads(array):
        return array.reshape(length, HEADS, HD).transpose(1, 0, 2)

    def one_head(operands):
        head_q, head_k, head_v = operands
        scores = jnp.dot(head_q, head_k.T, preferred_element_type=jnp.float32) * (1.0 / HD ** 0.5)
        probs = jax.nn.softmax(scores, axis=-1).astype(jnp.bfloat16)
        return jnp.dot(probs, head_v, preferred_element_type=jnp.float32).astype(jnp.bfloat16)
    heads_out = lax.map(one_head, (split_heads(queries), split_heads(keys_all), split_heads(values_all)))
    attended = heads_out.transpose(1, 0, 2).reshape(length, HEADS * HD)
    velocity = jnp.dot(attended, head_copy, preferred_element_type=jnp.float32)
    mean_next = latent.astype(jnp.float32) - velocity * (1.0 / STEPS)
    return (mean_next, attended)

def reference(latents, next_latents, noise, advantage, old_logp, timesteps, embed_weight, modulation, qkv_weight, head_weight):

    def sample(operands):
        latent, step_index, draw = operands
        mean_next, unused = forward(latent, step_index, qkv_weight[0], head_weight[0], embed_weight, modulation)
        return (mean_next + noise_level * draw.astype(jnp.float32)).astype(jnp.bfloat16)
    fresh = lax.map(sample, (latents[0], timesteps[0], noise))

    def learn(operands):
        latent, step_index, stored, gain, previous = operands
        mean_next, attended = forward(latent, step_index, qkv_weight[1], head_weight[1], embed_weight, modulation)
        residual = stored.astype(jnp.float32) - mean_next
        logp = -jnp.sum(residual * residual) / (2.0 * noise_level * noise_level * SEQ_LEN * CHANNELS)
        ratio = jnp.exp(logp - previous)
        weighted = (gain * ratio * residual).astype(jnp.bfloat16)
        return jnp.dot(attended.T, weighted, preferred_element_type=jnp.float32)
    terms = lax.map(learn, (latents[1], timesteps[1], next_latents, advantage, old_logp))
    gradient = lax.optimization_barrier(jnp.sum(terms, axis=0))
    mean_square = jnp.mean(gradient * gradient)
    updated = (head_weight[1].astype(jnp.float32) - step_size * gradient * lax.rsqrt(mean_square + update_eps)).astype(jnp.bfloat16)
    return (jnp.stack([fresh, fresh]), jnp.stack([updated, updated]))
```

```python
import functools
import math

import jax
import jax.numpy as jnp
from jax import lax
from jax.experimental import pallas as pl
from jax.experimental.pallas import tpu as pltpu
from jax.sharding import PartitionSpec as P

HD = 128
LANES = 128

noise_level = 0.8
step_size = 0.5
norm_eps = 1e-06
update_eps = 1e-06

bf16 = jnp.bfloat16
f32 = jnp.float32

VMEM = pl.BlockSpec(memory_space=pltpu.VMEM)
SMEM = pl.BlockSpec(memory_space=pltpu.SMEM)
PARAMS = pltpu.CompilerParams(vmem_limit_bytes=48 * 1024 * 1024)


def dot(a, b, precision=None):
    return lax.dot_general(
        a, b, (((1,), (0,)), ((), ())), precision=precision, preferred_element_type=f32
    )


def dot_nt(a, b, precision=None):
    return lax.dot_general(
        a, b, (((1,), (1,)), ((), ())), precision=precision, preferred_element_type=f32
    )


HIGHEST = lax.Precision.HIGHEST


def partial_kernel(
    steps_ref, place_ref, latent_ref, embed_ref, modulation_ref, weight_ref, sums_ref, scaled_ref, left_ref
):
    latent = latent_ref[...].astype(f32).T
    embedded = dot(latent.astype(bf16), embed_ref[...]).astype(bf16).astype(f32)
    width = embedded.shape[1]
    center = jnp.sum(embedded, axis=1, keepdims=True) * (1.0 / width)
    spread = jnp.sum((embedded - center) * (embedded - center), axis=1, keepdims=True) * (1.0 / width)
    scaled_ref[...] = (latent * lax.rsqrt(spread + norm_eps)).T

    channels, rows = embed_ref.shape[0], weight_ref.shape[1]
    rollouts = sums_ref.shape[0]
    block = channels + 16
    start = pl.multiple_of(place_ref[0] * rows, LANES)
    mean = jnp.sum(embed_ref[...].astype(f32), axis=1, keepdims=True) * (1.0 / width)
    centered = embed_ref[:, pl.ds(start, rows)].astype(f32) - mean
    row = lax.broadcasted_iota(jnp.int32, (16, rows), 0)
    for i in range(rollouts):
        step = steps_ref[i]
        shift = modulation_ref[step, 0:1, pl.ds(start, rows)]
        scale = modulation_ref[step, 1:2, pl.ds(start, rows)]
        high = shift.astype(bf16).astype(f32)
        tail = jnp.where(row == 0, high, jnp.where(row == 1, shift - high, 0.0))
        left_ref[i * block : i * block + channels, :] = (centered * (1.0 + scale)).astype(bf16)
        left_ref[i * block + channels : (i + 1) * block, :] = tail.astype(bf16)
    slot = lax.broadcasted_iota(jnp.int32, (16, LANES), 0)
    tails = [jnp.zeros((16, LANES), f32) for _ in range(rollouts)]
    for j in range(3):
        product = dot(left_ref[...], weight_ref[j])
        for i in range(rollouts):
            for h in range(2):
                c = 2 * j + h
                part = product[i * block : (i + 1) * block, h * HD : (h + 1) * HD]
                sums_ref[i, c * channels : (c + 1) * channels, :] = part[:channels].astype(bf16)
                offset = part[channels : channels + 1] + part[channels + 1 : channels + 2]
                high = offset.astype(bf16).astype(f32)
                tails[i] = jnp.where(slot == c, high, jnp.where(slot == c + 8, offset - high, tails[i]))
    for i in range(rollouts):
        sums_ref[i, 6 * channels : 6 * channels + 16, :] = tails[i].astype(bf16)


def absorb_kernel(sums_ref, head_ref, scaled_ref, pack_ref, values_ref, offsets_ref, *, factor, logit):
    channels = head_ref.shape[0]
    total = sums_ref[0].astype(f32)
    for i in range(1, sums_ref.shape[0]):
        total += sums_ref[i].astype(f32)
    total = total * factor
    blocks = [total[c * channels : (c + 1) * channels] for c in range(6)]
    offsets = total[6 * channels : 6 * channels + 8] + total[6 * channels + 8 : 6 * channels + 16]
    queries, keys, values = blocks[0:2], blocks[2:4], blocks[4:6]
    none = jnp.zeros((channels, LANES), f32)

    def beside(parts):
        return jnp.concatenate([parts[0], none], axis=0), jnp.concatenate([none, parts[1]], axis=0)

    heads = [head_ref[:, h * HD : (h + 1) * HD].astype(f32) for h in range(2)]
    query_pads, key_pads, value_pads = beside(queries), beside(keys), beside(values)
    bilinear = sum(dot_nt(keys[h], query_pads[h], HIGHEST) for h in range(2)) * logit
    outward = sum(dot_nt(heads[h], value_pads[h], HIGHEST) for h in range(2))
    pack_ref[0:channels, :] = scaled_ref[...].astype(bf16)
    pack_ref[channels : 2 * channels, :] = bilinear.astype(bf16)
    pack_ref[2 * channels : 3 * channels, :] = outward.astype(bf16)

    slot = lax.broadcasted_iota(jnp.int32, (8, LANES), 0)
    lane = lax.broadcasted_iota(jnp.int32, (8, LANES), 1)

    def pick(array, c):
        return jnp.sum(jnp.where(slot == c, array, 0.0), axis=0, keepdims=True)

    by_keys = [dot_nt(offsets, key_pads[h], HIGHEST) * logit for h in range(2)]
    by_queries = [dot_nt(offsets, query_pads[h], HIGHEST) * logit for h in range(2)]
    by_heads = [dot_nt(offsets, jnp.concatenate([heads[h], none], axis=0), HIGHEST) for h in range(2)]
    query_constant = pick(by_keys[0], 0) + pick(by_keys[1], 1)
    key_constant = pick(by_queries[0], 2) + pick(by_queries[1], 3)
    both = [
        jnp.sum(pick(offsets, h) * pick(offsets, 2 + h), axis=1, keepdims=True) * logit for h in range(2)
    ]
    outward_constant = pick(by_heads[0], 4) + pick(by_heads[1], 5)
    tail = jnp.where(slot == 0, query_constant, 0.0)
    tail = jnp.where(slot == 1, key_constant, tail)
    tail = jnp.where(slot == 2, jnp.where(lane < channels, both[0], both[1]), tail)
    tail = jnp.where(slot == 3, outward_constant, tail)
    pack_ref[3 * channels : 3 * channels + 16, :] = jnp.concatenate([tail, jnp.zeros_like(tail)], axis=0).astype(bf16)
    values_ref[0:channels, :] = values[0]
    values_ref[channels : 2 * channels, :] = values[1]
    offsets_ref[...] = offsets


def attend_kernel(
    pack_ref,
    scaled_ref,
    latent_ref,
    next_ref,
    noise_ref,
    fresh_ref,
    pieces_ref,
    keys_ref,
    values_ref,
    attended_ref,
    own_ref,
    velocity_ref,
    *,
    steps_count,
):
    blocks = pack_ref.shape[0]
    channels, tokens = latent_ref.shape
    length = blocks * tokens
    unit = (lax.broadcasted_iota(jnp.int32, (64, tokens), 0) == 0).astype(f32)
    constants = jnp.zeros((16, LANES), f32)
    for s in range(blocks):
        block = pack_ref[s, 0:channels, :]
        here = slice(s * tokens, (s + 1) * tokens)
        values_ref[0:channels, here] = block
        keys_ref[here, :] = jnp.concatenate([block.astype(f32), unit], axis=0).T.astype(bf16)
        constants += pack_ref[s, 3 * channels : 3 * channels + 16, :].astype(f32)
    values_ref[channels : channels + 16, :] = (
        lax.broadcasted_iota(jnp.int32, (16, length), 0) == 0
    ).astype(bf16)
    own = scaled_ref[...]
    none = jnp.zeros_like(own)
    own_ref[...] = jnp.concatenate(
        [jnp.concatenate([own, none], axis=1), jnp.concatenate([none, own], axis=1)], axis=0
    ).astype(bf16)
    velocity_ref[...] = jnp.zeros_like(velocity_ref)
    first = lax.broadcasted_iota(jnp.int32, (16, 2 * tokens), 0) == 0
    side = lax.broadcasted_iota(jnp.int32, (1, 2 * tokens), 1) < tokens
    rest = jnp.zeros((LANES - channels - 16, 2 * tokens), f32)

    def scores_of(s):
        own_pair = own_ref[...]
        queries = dot(pack_ref[s, channels : 2 * channels, :], own_pair)
        tail = pack_ref[s, 3 * channels : 3 * channels + 16, :]
        level = dot(tail, own_pair)[1:2, :]
        tail = tail.astype(f32)
        level += jnp.where(side, tail[2:3, 0:1], tail[2:3, channels : channels + 1])
        columns = jnp.concatenate([tail, jnp.zeros((LANES - 16, LANES), f32)], axis=0).T
        queries += jnp.concatenate(
            [
                jnp.broadcast_to(columns[0:channels, 0:1], (channels, tokens)),
                jnp.broadcast_to(columns[channels : 2 * channels, 0:1], (channels, tokens)),
            ],
            axis=1,
        )
        queries = jnp.concatenate([queries, jnp.where(first, level, 0.0), rest], axis=0).astype(bf16)
        return dot(keys_ref[...], queries)

    def finish(s, scores):
        top = jnp.max(scores, axis=0, keepdims=True)
        probs = jnp.exp2(scores - top).astype(bf16)
        sums = dot(values_ref[...], probs)
        normed = sums[0:channels] * (1.0 / sums[channels : channels + 1])
        stacked = jnp.concatenate([normed[:, :tokens], normed[:, tokens:]], axis=0).astype(bf16)
        attended_ref[s] = stacked
        velocity_ref[...] += dot(pack_ref[s, 2 * channels : 3 * channels, :], stacked)

    def body(s, carry):
        finish(s, scores_of(s))
        return carry

    lax.fori_loop(0, blocks, body, 0)

    velocity = velocity_ref[...] + jnp.concatenate(
        [constants, jnp.zeros((LANES - 16, LANES), f32)], axis=0
    ).T[0:channels, 3:4]
    mean_next = latent_ref[...].astype(f32) - velocity * (1.0 / steps_count)
    fresh_ref[...] = (mean_next + noise_level * noise_ref[...].astype(f32)).astype(bf16)
    residual = next_ref[...].astype(f32) - mean_next
    squared = jnp.sum(jnp.sum(residual * residual, axis=1, keepdims=True), axis=0, keepdims=True)
    residual = residual.astype(bf16)
    wide = jnp.concatenate([residual, jnp.zeros((LANES - channels, tokens), bf16)], axis=0)
    column_sums = dot_nt(jnp.ones((16, tokens), bf16), wide)
    slot = lax.broadcasted_iota(jnp.int32, (16, LANES), 0)
    high = squared.astype(bf16).astype(f32)
    tail = jnp.where(slot == 0, column_sums, jnp.where(slot == 1, high, jnp.where(slot == 2, squared - high, 0.0)))
    tail = tail.astype(bf16)
    for s in range(blocks):
        pieces_ref[s, 0:channels, :] = dot_nt(residual, attended_ref[s]).astype(bf16)
        pieces_ref[s, channels : channels + 16, :] = tail


def gradient_kernel(pieces_ref, values_ref, offsets_ref, gain_ref, old_ref, out_ref, *, entries):
    total = pieces_ref[0].astype(f32)
    for s in range(1, pieces_ref.shape[0]):
        total += pieces_ref[s].astype(f32)
    channels = out_ref.shape[1]
    tail = total[channels : channels + 16]
    squared = tail[1:2, 0:1] + tail[2:3, 0:1]
    logp = -squared / (2.0 * noise_level * noise_level * entries)
    scale = gain_ref[0] * jnp.exp(logp - old_ref[0])
    column = jnp.concatenate([tail, jnp.zeros((LANES - 16, LANES), f32)], axis=0).T[0:channels, 0:1]
    product = total[0:channels]
    none = jnp.zeros((channels, LANES), f32)
    parts = []
    for h in range(2):
        values = values_ref[h * channels : (h + 1) * channels, :]
        padded = jnp.concatenate([values, none] if h == 0 else [none, values], axis=0)
        parts.append(dot(product, padded, HIGHEST) + column * offsets_ref[4 + h : 5 + h, :])
    gradient = jnp.concatenate(parts, axis=1) * scale
    for i in range(out_ref.shape[0]):
        out_ref[i] = gradient


def total_kernel(parts_ref, gradient_ref, squares_ref):
    gradient = parts_ref[0]
    for i in range(1, parts_ref.shape[0]):
        gradient += parts_ref[i]
    gradient_ref[...] = gradient
    squares = jnp.sum(gradient * gradient, axis=0, keepdims=True)
    squares = squares[:, 0:LANES] + squares[:, LANES:]
    for s in range(squares_ref.shape[0]):
        squares_ref[s] = squares


def update_kernel(gradient_ref, squares_ref, head_ref, out_ref, *, entries):
    squares = squares_ref[0]
    for s in range(1, squares_ref.shape[0]):
        squares += squares_ref[s]
    mean_square = jnp.sum(squares, axis=1, keepdims=True) * (1.0 / entries)
    change = step_size * gradient_ref[...] * lax.rsqrt(mean_square + update_eps)
    out_ref[...] = (head_ref[...].astype(f32) - change).astype(bf16)


def call(kernel, outs, specs, scratch=()):
    single = not isinstance(outs, (list, tuple))
    return pl.pallas_call(
        kernel,
        out_shape=outs,
        in_specs=specs,
        out_specs=VMEM if single else [VMEM] * len(outs),
        scratch_shapes=list(scratch),
        compiler_params=PARAMS,
    )


def shape(*dims, dtype=f32):
    return jax.ShapeDtypeStruct(dims, dtype)


def on_device(
    latents,
    next_latents,
    noise,
    advantage,
    old_logp,
    timesteps,
    embed_weight,
    modulation,
    qkv_weight,
    head_weight,
):
    role_id = lax.axis_index("role")
    rollouts, blocks = lax.axis_size("dp"), lax.axis_size("seq")
    latent = latents[0, 0].T
    channels, tokens = latent.shape
    width = modulation.shape[2]
    steps_count = modulation.shape[0]
    rows = qkv_weight.shape[2]
    columns = qkv_weight.shape[3]
    head = head_weight[0].T

    steps = lax.all_to_all(
        jnp.broadcast_to(timesteps.reshape(1, 1, 1), (rollouts, 1, LANES)), "dp", 0, 0
    )[:, 0, 0]
    place = lax.axis_index("dp").reshape(1)
    sums, scaled = call(
        partial_kernel,
        [shape(rollouts, 6 * channels + 16, LANES, dtype=bf16), shape(channels, tokens)],
        [SMEM, SMEM] + [VMEM] * 4,
        [pltpu.VMEM((rollouts * (channels + 16), rows), bf16)],
    )(steps, place, latent, embed_weight, modulation, qkv_weight[0])
    sums = lax.all_to_all(sums, "dp", 0, 0)
    pack, values, offsets = call(
        functools.partial(absorb_kernel, factor=width**-0.5, logit=math.log2(math.e) / HD**0.5),
        [shape(3 * channels + 16, LANES, dtype=bf16), shape(2 * channels, HD), shape(8, HD)],
        [VMEM] * 3,
    )(sums, head, scaled)
    packs = lax.all_gather(pack, "seq", axis=0, tiled=False)
    fresh, pieces = call(
        functools.partial(attend_kernel, steps_count=steps_count),
        [shape(channels, tokens, dtype=bf16), shape(blocks, channels + 16, LANES, dtype=bf16)],
        [VMEM] * 5,
        [
            pltpu.VMEM((blocks * tokens, LANES), bf16),
            pltpu.VMEM((channels + 16, blocks * tokens), bf16),
            pltpu.VMEM((blocks, 2 * channels, tokens), bf16),
            pltpu.VMEM((2 * channels, 2 * tokens), bf16),
            pltpu.VMEM((channels, tokens), f32),
        ],
    )(packs, scaled, latent, next_latents[0].T, noise[0].T)
    fresh_received = lax.ppermute(fresh, "role", [(0, 1)])
    pieces = lax.all_to_all(pieces, "seq", 0, 0)
    parts = call(
        functools.partial(gradient_kernel, entries=tokens * blocks * channels),
        shape(rollouts, channels, columns),
        [VMEM, VMEM, VMEM, SMEM, SMEM],
    )(pieces, values, offsets, advantage, old_logp)
    parts = lax.all_to_all(parts, "dp", 0, 0)
    gradient, squares = call(
        total_kernel,
        [shape(channels, columns), shape(blocks, 1, LANES)],
        [VMEM],
    )(parts)
    squares = lax.all_to_all(squares, "seq", 0, 0)
    updated = call(
        functools.partial(update_kernel, entries=columns * blocks * channels),
        shape(channels, columns, dtype=bf16),
        [VMEM] * 3,
    )(gradient, squares, head)
    weight_received = lax.ppermute(updated, "role", [(1, 0)])
    fresh_out = jnp.where(role_id == 0, fresh, fresh_received).T
    weight_out = jnp.where(role_id == 1, updated, weight_received).T
    return (fresh_out[None, None], weight_out[None])


def solution(mesh):
    in_specs = (
        P("role", "dp", "seq", None),
        P("dp", "seq", None),
        P("dp", "seq", None),
        P("dp"),
        P("dp"),
        P("role", "dp"),
        P(),
        P(),
        P("role", None, "dp", "seq"),
        P("role", "seq", None),
    )
    out_specs = (P("role", "dp", "seq", None), P("role", "seq", None))
    return jax.shard_map(
        on_device, mesh=mesh, in_specs=in_specs, out_specs=out_specs, check_vma=False
    )
```

```python
import functools
import math

import jax
import jax.numpy as jnp
from jax import lax
from jax.experimental import pallas as pl
from jax.experimental.pallas import tpu as pltpu
from jax.sharding import PartitionSpec as P

HD = 128
LANES = 128
CORES = 2

noise_level = 0.8
step_size = 0.5
norm_eps = 1e-06
update_eps = 1e-06

bf16 = jnp.bfloat16
f32 = jnp.float32

VMEM = pl.BlockSpec(memory_space=pltpu.VMEM)
SMEM = pl.BlockSpec(memory_space=pltpu.SMEM)
HBM = pl.BlockSpec(memory_space=pltpu.HBM)


def dot(a, b, precision=None):
    return lax.dot_general(
        a, b, (((1,), (0,)), ((), ())), precision=precision, preferred_element_type=f32
    )


def dot_nt(a, b, precision=None):
    return lax.dot_general(
        a, b, (((1,), (1,)), ((), ())), precision=precision, preferred_element_type=f32
    )


HIGHEST = lax.Precision.HIGHEST


def token_kernel(place_ref, latent_ref, next_ref, noise_ref, embed_ref, tokens_ref, centered_ref, ahead_ref, drawn_ref):
    latent = latent_ref[...].astype(f32)
    ahead_ref[...] = next_ref[...].astype(f32) - latent
    drawn_ref[...] = latent + noise_level * noise_ref[...].astype(f32)
    embed = embed_ref[...]
    embedded = dot(latent.T.astype(bf16), embed).astype(bf16).astype(f32)
    width = embedded.shape[1]
    center = jnp.sum(embedded, axis=1, keepdims=True) * (1.0 / width)
    spread = jnp.sum((embedded - center) * (embedded - center), axis=1, keepdims=True) * (1.0 / width)
    tokens_ref[...] = (latent.T * lax.rsqrt(spread + norm_eps)).T.astype(bf16)
    mean = jnp.sum(embed.astype(f32), axis=1, keepdims=True) * (1.0 / width)
    rows = centered_ref.shape[1]
    start = pl.multiple_of(place_ref[0] * rows, LANES)
    centered_ref[...] = embed_ref[:, pl.ds(start, rows)].astype(f32) - mean


def partial_kernel(place_ref, centered_ref, modulation_ref, weight_ref, sums_ref, left_ref):
    channels, rows = centered_ref.shape
    steps = sums_ref.shape[0]
    block = channels + 16
    start = pl.multiple_of(place_ref[0] * rows, LANES)
    centered = centered_ref[...]
    row = lax.broadcasted_iota(jnp.int32, (16, rows), 0)
    for i in range(steps):
        shift = modulation_ref[i, 0:1, pl.ds(start, rows)]
        scale = modulation_ref[i, 1:2, pl.ds(start, rows)]
        high = shift.astype(bf16).astype(f32)
        tail = jnp.where(row == 0, high, jnp.where(row == 1, shift - high, 0.0))
        left_ref[i * block : i * block + channels, :] = (centered * (1.0 + scale)).astype(bf16)
        left_ref[i * block + channels : (i + 1) * block, :] = tail.astype(bf16)
    slot = lax.broadcasted_iota(jnp.int32, (16, LANES), 0)
    tails = [jnp.zeros((16, LANES), f32) for _ in range(steps)]
    for j in range(3):
        product = dot(left_ref[...], weight_ref[j])
        for i in range(steps):
            for h in range(2):
                c = 2 * j + h
                part = product[i * block : (i + 1) * block, h * HD : (h + 1) * HD]
                sums_ref[i, c * channels : (c + 1) * channels, :] = part[:channels].astype(bf16)
                offset = part[channels : channels + 1] + part[channels + 1 : channels + 2]
                high = offset.astype(bf16).astype(f32)
                tails[i] = jnp.where(slot == c, high, jnp.where(slot == c + 8, offset - high, tails[i]))
    for i in range(steps):
        sums_ref[i, 6 * channels : 6 * channels + 16, :] = tails[i].astype(bf16)


def step_kernel(step_ref, out_ref):
    out_ref[...] = jnp.broadcast_to(step_ref[0, 0], out_ref.shape)


def choose_kernel(steps_ref, sums_ref, out_ref):
    for i in range(out_ref.shape[0]):
        out_ref[i] = sums_ref[steps_ref[i]]


def absorb_kernel(sums_ref, head_ref, pack_ref, values_ref, offsets_ref, *, factor, logit):
    channels = head_ref.shape[0]
    total = sums_ref[0].astype(f32)
    for i in range(1, sums_ref.shape[0]):
        total += sums_ref[i].astype(f32)
    total = total * factor
    blocks = [total[c * channels : (c + 1) * channels] for c in range(6)]
    offsets = total[6 * channels : 6 * channels + 8] + total[6 * channels + 8 : 6 * channels + 16]
    queries, keys, values = blocks[0:2], blocks[2:4], blocks[4:6]
    none = jnp.zeros((channels, LANES), f32)

    def beside(parts):
        return jnp.concatenate([parts[0], none], axis=0), jnp.concatenate([none, parts[1]], axis=0)

    heads = [head_ref[:, h * HD : (h + 1) * HD].astype(f32) for h in range(2)]
    query_pads, key_pads, value_pads = beside(queries), beside(keys), beside(values)
    bilinear = sum(dot_nt(keys[h], query_pads[h], HIGHEST) for h in range(2)) * logit
    outward = sum(dot_nt(heads[h], value_pads[h], HIGHEST) for h in range(2))

    slot = lax.broadcasted_iota(jnp.int32, (8, LANES), 0)
    lane = lax.broadcasted_iota(jnp.int32, (8, LANES), 1)

    def pick(array, c):
        return jnp.sum(jnp.where(slot == c, array, 0.0), axis=0, keepdims=True)

    by_keys = [dot_nt(offsets, key_pads[h], HIGHEST) * logit for h in range(2)]
    by_queries = [dot_nt(offsets, query_pads[h], HIGHEST) * logit for h in range(2)]
    by_heads = [dot_nt(offsets, jnp.concatenate([heads[h], none], axis=0), HIGHEST) for h in range(2)]
    query_constant = pick(by_keys[0], 0) + pick(by_keys[1], 1)
    key_constant = pick(by_queries[0], 2) + pick(by_queries[1], 3)
    both = [
        jnp.sum(pick(offsets, h) * pick(offsets, 2 + h), axis=1, keepdims=True) * logit for h in range(2)
    ]
    outward_constant = pick(by_heads[0], 4) + pick(by_heads[1], 5)
    tail = jnp.where(slot == 0, query_constant, 0.0)
    tail = jnp.where(slot == 1, key_constant, tail)
    tail = jnp.where(slot == 2, jnp.where(lane < channels, both[0], both[1]), tail)
    tail = jnp.where(slot == 3, outward_constant, tail)
    pack = jnp.concatenate([bilinear, outward, tail, jnp.zeros_like(tail)], axis=0).astype(bf16)
    for z in range(pack_ref.shape[0]):
        pack_ref[z] = pack
    values_ref[0:channels, :] = values[0]
    values_ref[channels : 2 * channels, :] = values[1]
    offsets_ref[...] = offsets


def tokens_kernel(core_ref, near_ref, far_ref, keys_ref, values_ref, own_ref):
    half, channels, tokens = near_ref.shape
    unit = (lax.broadcasted_iota(jnp.int32, (LANES - channels, tokens), 0) == 0).astype(f32)
    for s in range(2 * half):
        block = near_ref[s] if s < half else far_ref[s - half]
        here = slice(s * tokens, (s + 1) * tokens)
        values_ref[0:channels, here] = block
        keys_ref[here, :] = jnp.concatenate([block.astype(f32), unit], axis=0).T.astype(bf16)
    values_ref[channels : channels + 16, :] = (
        lax.broadcasted_iota(jnp.int32, (16, 2 * half * tokens), 0) == 0
    ).astype(bf16)
    own_ref[...] = jnp.zeros_like(own_ref)
    for c in range(CORES):
        block = jnp.where(core_ref[0] == c, near_ref[0], near_ref[1])
        for p in range(2):
            left = (CORES * p + c) * tokens
            own_ref[p * channels : (p + 1) * channels, left : left + tokens] = block


def attend_kernel(
    pack_ref,
    keys_ref,
    values_ref,
    own_ref,
    ahead_ref,
    shared_ref,
    attended_ref,
    outward_ref,
    queries_ref,
    scores_ref,
    top_ref,
):
    pairs = pack_ref.shape[0]
    heads = 2 * pairs
    channels, tokens = ahead_ref.shape
    length = keys_ref.shape[0]
    wide = CORES * tokens

    own = own_ref[...]
    tails = pack_ref[:, 2 * channels : 2 * channels + 16, :]
    levels = dot(tails.reshape(pairs * 16, LANES), own)
    tails = tails.astype(f32)
    constants = jnp.concatenate(
        [tails[s, 0:1] for s in range(pairs)]
        + [jnp.sum(tails, axis=0), jnp.zeros((LANES - 16 - pairs, LANES), f32)],
        axis=0,
    ).T
    queries = dot(pack_ref[:, 0:channels, :].reshape(pairs * channels, LANES), own)
    first = lax.broadcasted_iota(jnp.int32, (16, wide), 0) == 0
    for s in range(pairs):
        outward_ref[:, s * LANES : (s + 1) * LANES] = pack_ref[s, channels : 2 * channels, :]
        for p in range(2):
            here = slice(p * wide, (p + 1) * wide)
            shift = constants[p * channels : (p + 1) * channels, s : s + 1]
            level = levels[16 * s + 1 : 16 * s + 2, here] + tails[s, 2:3, p * channels : p * channels + 1]
            queries_ref[2 * s + p, 0:channels, :] = (
                queries[s * channels : (s + 1) * channels, here] + shift
            ).astype(bf16)
            queries_ref[2 * s + p, channels : channels + 16, :] = jnp.where(first, level, 0.0).astype(bf16)
            queries_ref[2 * s + p, channels + 16 :, :] = jnp.zeros((LANES - channels - 16, wide), bf16)

    part = 256

    def start(slot, h):
        query = queries_ref[h]
        top = None
        for c in range(length // part):
            scores = dot(keys_ref[c * part : (c + 1) * part, :], query)
            scores_ref[slot, c * part : (c + 1) * part, :] = scores
            high = jnp.max(scores.reshape(part // 8, 8, wide), axis=0)
            top = high if top is None else jnp.maximum(top, high)
        top_ref[slot] = top

    def finish(slot, h):
        top = jnp.max(top_ref[slot], axis=0, keepdims=True)
        probs = jnp.exp2(scores_ref[slot] - top).astype(bf16)
        sums = dot(values_ref[...], probs)
        attended_ref[h] = (sums[0:channels] * (1.0 / sums[channels : channels + 1])).astype(bf16)

    start(0, 0)

    def body(i, carry):
        start(1, 2 * i + 1)
        finish(0, 2 * i)
        start(0, lax.rem(2 * i + 2, heads))
        finish(1, 2 * i + 1)
        return carry

    lax.fori_loop(0, pairs, body, 0, unroll=2)

    shared_ref[:, 0:wide] = (
        dot(outward_ref[...], attended_ref[...].reshape(heads * channels, wide))
        + constants[0:channels, pairs + 3 : pairs + 4]
    )
    shared_ref[:, wide:] = ahead_ref[...]


def finish_kernel(
    core_ref, mine_ref, other_ref, attended_ref, drawn_ref, fresh_ref, pieces_ref, *, steps_count
):
    channels, tokens = drawn_ref.shape
    wide = CORES * tokens
    is_first = core_ref[0] == 0
    change = (mine_ref[:, 0:wide] + other_ref[:, 0:wide]) * (1.0 / steps_count)
    mine, other = mine_ref[:, wide:], other_ref[:, wide:]
    residual = change + jnp.concatenate(
        [jnp.where(is_first, mine, other), jnp.where(is_first, other, mine)], axis=1
    )
    own = jnp.where(is_first, change[:, 0:tokens], change[:, tokens:])
    fresh_ref[...] = (drawn_ref[...] - own).astype(bf16)
    squared = jnp.sum(jnp.sum(residual * residual, axis=1, keepdims=True), axis=0, keepdims=True)
    residual = residual.astype(bf16)
    padded = jnp.concatenate([residual, jnp.zeros((LANES - channels, wide), bf16)], axis=0)
    column_sums = dot_nt(jnp.ones((16, wide), bf16), padded)
    slot = lax.broadcasted_iota(jnp.int32, (16, LANES), 0)
    high = squared.astype(bf16).astype(f32)
    tail = jnp.where(slot == 0, column_sums, jnp.where(slot == 1, high, jnp.where(slot == 2, squared - high, 0.0)))
    tail = tail.astype(bf16)
    attended = attended_ref[...]
    product = dot_nt(residual, attended.reshape(attended.shape[0] * channels, wide)).astype(bf16)
    for s in range(pieces_ref.shape[0]):
        pieces_ref[s, 0:channels, :] = product[:, s * LANES : (s + 1) * LANES]
        pieces_ref[s, channels : channels + 16, :] = tail


def gradient_kernel(pieces_ref, values_ref, offsets_ref, gain_ref, old_ref, out_ref, *, entries):
    total = pieces_ref[0].astype(f32)
    for s in range(1, pieces_ref.shape[0]):
        total += pieces_ref[s].astype(f32)
    channels = out_ref.shape[1]
    tail = total[channels : channels + 16]
    squared = tail[1:2, 0:1] + tail[2:3, 0:1]
    logp = -squared / (2.0 * noise_level * noise_level * entries)
    scale = gain_ref[0] * jnp.exp(logp - old_ref[0])
    column = jnp.concatenate([tail, jnp.zeros((LANES - 16, LANES), f32)], axis=0).T[0:channels, 0:1]
    product = total[0:channels]
    none = jnp.zeros((channels, LANES), f32)
    parts = []
    for h in range(2):
        values = values_ref[h * channels : (h + 1) * channels, :]
        padded = jnp.concatenate([values, none] if h == 0 else [none, values], axis=0)
        parts.append(dot(product, padded, HIGHEST) + column * offsets_ref[4 + h : 5 + h, :])
    gradient = (jnp.concatenate(parts, axis=1) * scale).astype(bf16)
    for i in range(out_ref.shape[0]):
        out_ref[i] = gradient


def total_kernel(parts_ref, gradient_ref, squares_ref):
    gradient = parts_ref[0].astype(f32)
    for i in range(1, parts_ref.shape[0]):
        gradient += parts_ref[i].astype(f32)
    gradient_ref[...] = gradient
    squares = jnp.sum(gradient * gradient, axis=0, keepdims=True)
    squares = squares[:, 0:LANES] + squares[:, LANES:]
    for s in range(squares_ref.shape[0]):
        squares_ref[s] = squares


def update_kernel(role_ref, gradient_ref, squares_ref, head_ref, fresh_ref, out_ref, *, entries):
    squares = squares_ref[0]
    for s in range(1, squares_ref.shape[0]):
        squares += squares_ref[s]
    mean_square = jnp.sum(squares, axis=1, keepdims=True) * (1.0 / entries)
    change = step_size * gradient_ref[...] * lax.rsqrt(mean_square + update_eps)
    fresh = fresh_ref[...]
    fresh = jnp.concatenate([fresh, jnp.zeros_like(fresh)], axis=1)
    out_ref[...] = jnp.where(role_ref[0] == 1, (head_ref[...].astype(f32) - change).astype(bf16), fresh)


def output_kernel(role_ref, mine_ref, other_ref, fresh_ref, head_ref):
    learner = role_ref[0] == 1
    mine, other = mine_ref[...], other_ref[...]
    head_ref[...] = jnp.where(learner, mine, other)
    fresh_ref[...] = jnp.where(learner, other, mine)[:, 0 : fresh_ref.shape[1]]


def call(kernel, outs, specs, scratch=(), flops=0, mib=32, place=VMEM):
    single = not isinstance(outs, (list, tuple))
    return pl.pallas_call(
        kernel,
        out_shape=outs,
        in_specs=specs,
        out_specs=place if single else [place] * len(outs),
        scratch_shapes=list(scratch),
        compiler_params=pltpu.CompilerParams(vmem_limit_bytes=mib * 1024 * 1024),
        cost_estimate=pl.CostEstimate(flops=flops, bytes_accessed=0, transcendentals=0),
    )


def shape(*dims, dtype=f32):
    return jax.ShapeDtypeStruct(dims, dtype)


def on_device(
    latents,
    next_latents,
    noise,
    advantage,
    old_logp,
    timesteps,
    embed_weight,
    modulation,
    qkv_weight,
    head_weight,
):
    core = (lax.axis_index("seq") % CORES).reshape(1)
    rollouts, blocks = lax.axis_size("dp"), lax.axis_size("seq")
    chips = blocks // CORES
    along = [[CORES * z + c for z in range(chips)] for c in range(CORES)]
    swap = [(i, i ^ 1) for i in range(blocks)]
    latent = latents[0, 0].T
    channels, tokens = latent.shape
    steps_count, _, width = modulation.shape
    rows, columns = qkv_weight.shape[2:]
    wide = CORES * tokens
    head = head_weight[0].T

    steps = call(step_kernel, shape(rollouts, 1, LANES, dtype=jnp.int32), [SMEM], mib=1)(timesteps)
    steps = lax.all_to_all(steps, "dp", 0, 0)[:, 0, 0]
    place = lax.axis_index("dp").reshape(1)
    near, centered, ahead, drawn = call(
        token_kernel,
        [
            shape(channels, tokens, dtype=bf16),
            shape(channels, rows),
            shape(channels, tokens),
            shape(channels, tokens),
        ],
        [SMEM] + [VMEM] * 4,
        flops=10**9,
        mib=16,
    )(place, latent, next_latents[0].T, noise[0].T, embed_weight)

    def across(value, bits):
        return lax.ppermute(value, "seq", [(i, i ^ bits) for i in range(blocks)])

    near = jnp.stack([near, across(near, 1)])
    near = jnp.concatenate([near] + [across(near, bits) for bits in (8, 4, 12)], axis=0)
    sums = call(
        partial_kernel,
        shape(steps_count, 6 * channels + 16, LANES, dtype=bf16),
        [SMEM] + [VMEM] * 3,
        [pltpu.VMEM((steps_count * (channels + 16), rows), bf16)],
        flops=3 * 10**9,
        mib=16,
    )(place, centered, modulation, qkv_weight[0])
    sums = call(
        choose_kernel, shape(rollouts, 6 * channels + 16, LANES, dtype=bf16), [SMEM, VMEM], mib=16
    )(steps, sums)

    far = across(near, 2)
    sums = lax.all_to_all(sums, "dp", 0, 0)
    pack, values, offsets = call(
        functools.partial(absorb_kernel, factor=width**-0.5, logit=math.log2(math.e) / HD**0.5),
        [shape(chips, 2 * channels + 16, LANES, dtype=bf16), shape(2 * channels, HD), shape(8, HD)],
        [VMEM] * 2,
    )(sums, head)
    pack, far = lax.optimization_barrier((pack, far))
    packs = lax.all_to_all(pack, "seq", 0, 0, axis_index_groups=along)
    keys, spread, own = call(
        tokens_kernel,
        [
            shape(blocks * tokens, LANES, dtype=bf16),
            shape(channels + 16, blocks * tokens, dtype=bf16),
            shape(2 * channels, 2 * wide, dtype=bf16),
        ],
        [SMEM, VMEM, VMEM],
        flops=10**9,
    )(core, near, far)
    shared, attended = call(
        attend_kernel,
        [shape(channels, wide + tokens), shape(2 * chips, channels, wide, dtype=bf16)],
        [VMEM] * 5,
        [
            pltpu.VMEM((channels, chips * LANES), bf16),
            pltpu.VMEM((2 * chips, LANES, wide), bf16),
            pltpu.VMEM((2, blocks * tokens, wide), f32),
            pltpu.VMEM((2, 8, wide), f32),
        ],
    )(packs, keys, spread, own, ahead)
    other = lax.ppermute(shared, "seq", swap)
    fresh, pieces = call(
        functools.partial(finish_kernel, steps_count=steps_count),
        [shape(channels, tokens, dtype=bf16), shape(chips, channels + 16, LANES, dtype=bf16)],
        [SMEM] + [VMEM] * 4,
    )(core, shared, other, attended, drawn)
    pieces = lax.all_to_all(pieces, "seq", 0, 0, axis_index_groups=along)
    parts = call(
        functools.partial(gradient_kernel, entries=tokens * blocks * channels),
        shape(rollouts, channels, columns, dtype=bf16),
        [VMEM, VMEM, VMEM, SMEM, SMEM],
    )(pieces, values, offsets, advantage, old_logp)
    parts = lax.all_to_all(parts, "dp", 0, 0)
    gradient, squares = call(
        total_kernel,
        [shape(channels, columns), shape(blocks, 1, LANES)],
        [VMEM],
    )(parts)
    squares = lax.all_to_all(squares, "seq", 0, 0)
    role = lax.axis_index("role").reshape(1)
    mine = call(
        functools.partial(update_kernel, entries=columns * blocks * channels),
        shape(channels, columns, dtype=bf16),
        [SMEM] + [VMEM] * 4,
    )(role, gradient, squares, head, fresh)
    other = lax.ppermute(mine, "role", [(0, 1), (1, 0)])
    fresh_out, head_out = call(
        output_kernel,
        [shape(channels, tokens, dtype=bf16), shape(channels, columns, dtype=bf16)],
        [SMEM, VMEM, VMEM],
    )(role, mine, other)
    return (fresh_out.T[None, None], head_out.T[None])


def solution(mesh):
    in_specs = (
        P("role", "dp", "seq", None),
        P("dp", "seq", None),
        P("dp", "seq", None),
        P("dp"),
        P("dp"),
        P("role", "dp"),
        P(),
        P(),
        P("role", None, "dp", "seq"),
        P("role", "seq", None),
    )
    out_specs = (P("role", "dp", "seq", None), P("role", "seq", None))
    return jax.shard_map(
        on_device, mesh=mesh, in_specs=in_specs, out_specs=out_specs, check_vma=False
    )
```

```python
import functools
import math

import jax
import jax.numpy as jnp
from jax import lax
from jax.experimental import pallas as pl
from jax.experimental.pallas import tpu as pltpu
from jax.sharding import PartitionSpec as P

HD = 128
LANES = 128
CORES = 2

noise_level = 0.8
step_size = 0.5
norm_eps = 1e-06
update_eps = 1e-06

bf16 = jnp.bfloat16
f32 = jnp.float32

VMEM = pl.BlockSpec(memory_space=pltpu.VMEM)
SMEM = pl.BlockSpec(memory_space=pltpu.SMEM)
HBM = pl.BlockSpec(memory_space=pltpu.HBM)


def dot(a, b, precision=None):
    return lax.dot_general(
        a, b, (((1,), (0,)), ((), ())), precision=precision, preferred_element_type=f32
    )


def dot_nt(a, b, precision=None):
    return lax.dot_general(
        a, b, (((1,), (1,)), ((), ())), precision=precision, preferred_element_type=f32
    )


HIGHEST = lax.Precision.HIGHEST


def token_kernel(place_ref, latent_ref, next_ref, noise_ref, embed_ref, tokens_ref, centered_ref, ahead_ref, drawn_ref):
    latent = latent_ref[...].astype(f32)
    ahead_ref[...] = next_ref[...].astype(f32) - latent
    drawn_ref[...] = latent + noise_level * noise_ref[...].astype(f32)
    embed = embed_ref[...]
    embedded = dot(latent.T.astype(bf16), embed).astype(bf16).astype(f32)
    width = embedded.shape[1]
    center = jnp.sum(embedded, axis=1, keepdims=True) * (1.0 / width)
    spread = jnp.sum((embedded - center) * (embedded - center), axis=1, keepdims=True) * (1.0 / width)
    tokens_ref[...] = (latent.T * lax.rsqrt(spread + norm_eps)).T.astype(bf16)
    mean = jnp.sum(embed.astype(f32), axis=1, keepdims=True) * (1.0 / width)
    rows = centered_ref.shape[1]
    start = pl.multiple_of(place_ref[0] * rows, LANES)
    centered_ref[...] = embed_ref[:, pl.ds(start, rows)].astype(f32) - mean


def partial_kernel(place_ref, centered_ref, modulation_ref, weight_ref, sums_ref, left_ref):
    channels, rows = centered_ref.shape
    steps = sums_ref.shape[0]
    block = channels + 16
    start = pl.multiple_of(place_ref[0] * rows, LANES)
    centered = centered_ref[...]
    row = lax.broadcasted_iota(jnp.int32, (16, rows), 0)
    for i in range(steps):
        shift = modulation_ref[i, 0:1, pl.ds(start, rows)]
        scale = modulation_ref[i, 1:2, pl.ds(start, rows)]
        high = shift.astype(bf16).astype(f32)
        tail = jnp.where(row == 0, high, jnp.where(row == 1, shift - high, 0.0))
        left_ref[i * block : i * block + channels, :] = (centered * (1.0 + scale)).astype(bf16)
        left_ref[i * block + channels : (i + 1) * block, :] = tail.astype(bf16)
    slot = lax.broadcasted_iota(jnp.int32, (16, LANES), 0)
    tails = [jnp.zeros((16, LANES), f32) for _ in range(steps)]
    for j in range(3):
        product = dot(left_ref[...], weight_ref[j])
        for i in range(steps):
            for h in range(2):
                c = 2 * j + h
                part = product[i * block : (i + 1) * block, h * HD : (h + 1) * HD]
                sums_ref[i, c * channels : (c + 1) * channels, :] = part[:channels].astype(bf16)
                offset = part[channels : channels + 1] + part[channels + 1 : channels + 2]
                high = offset.astype(bf16).astype(f32)
                tails[i] = jnp.where(slot == c, high, jnp.where(slot == c + 8, offset - high, tails[i]))
    for i in range(steps):
        sums_ref[i, 6 * channels : 6 * channels + 16, :] = tails[i].astype(bf16)


def step_kernel(step_ref, out_ref):
    out_ref[...] = jnp.broadcast_to(step_ref[0, 0], out_ref.shape)


def choose_kernel(steps_ref, sums_ref, out_ref):
    for i in range(out_ref.shape[0]):
        out_ref[i] = sums_ref[steps_ref[i]]


def absorb_kernel(sums_ref, head_ref, pack_ref, values_ref, offsets_ref, *, factor, logit):
    channels = head_ref.shape[0]
    total = sums_ref[0].astype(f32)
    for i in range(1, sums_ref.shape[0]):
        total += sums_ref[i].astype(f32)
    total = total * factor
    blocks = [total[c * channels : (c + 1) * channels] for c in range(6)]
    offsets = total[6 * channels : 6 * channels + 8] + total[6 * channels + 8 : 6 * channels + 16]
    queries, keys, values = blocks[0:2], blocks[2:4], blocks[4:6]
    none = jnp.zeros((channels, LANES), f32)

    def beside(parts):
        return jnp.concatenate([parts[0], none], axis=0), jnp.concatenate([none, parts[1]], axis=0)

    heads = [head_ref[:, h * HD : (h + 1) * HD].astype(f32) for h in range(2)]
    query_pads, key_pads, value_pads = beside(queries), beside(keys), beside(values)
    bilinear = sum(dot_nt(keys[h], query_pads[h], HIGHEST) for h in range(2)) * logit
    outward = sum(dot_nt(heads[h], value_pads[h], HIGHEST) for h in range(2))

    slot = lax.broadcasted_iota(jnp.int32, (8, LANES), 0)
    lane = lax.broadcasted_iota(jnp.int32, (8, LANES), 1)

    def pick(array, c):
        return jnp.sum(jnp.where(slot == c, array, 0.0), axis=0, keepdims=True)

    by_keys = [dot_nt(offsets, key_pads[h], HIGHEST) * logit for h in range(2)]
    by_queries = [dot_nt(offsets, query_pads[h], HIGHEST) * logit for h in range(2)]
    by_heads = [dot_nt(offsets, jnp.concatenate([heads[h], none], axis=0), HIGHEST) for h in range(2)]
    query_constant = pick(by_keys[0], 0) + pick(by_keys[1], 1)
    key_constant = pick(by_queries[0], 2) + pick(by_queries[1], 3)
    both = [
        jnp.sum(pick(offsets, h) * pick(offsets, 2 + h), axis=1, keepdims=True) * logit for h in range(2)
    ]
    outward_constant = pick(by_heads[0], 4) + pick(by_heads[1], 5)
    tail = jnp.where(slot == 0, query_constant, 0.0)
    tail = jnp.where(slot == 1, key_constant, tail)
    tail = jnp.where(slot == 2, jnp.where(lane < channels, both[0], both[1]), tail)
    tail = jnp.where(slot == 3, outward_constant, tail)
    pack_ref[0] = jnp.concatenate([bilinear, outward, tail, jnp.zeros_like(tail)], axis=0).astype(bf16)
    values_ref[0:channels, :] = values[0]
    values_ref[channels : 2 * channels, :] = values[1]
    offsets_ref[...] = offsets


def tokens_kernel(core_ref, near_ref, far_ref, keys_ref, values_ref, own_ref):
    half, channels, tokens = near_ref.shape
    unit = (lax.broadcasted_iota(jnp.int32, (LANES - channels, tokens), 0) == 0).astype(f32)
    for s in range(2 * half):
        block = near_ref[s] if s < half else far_ref[s - half]
        here = slice(s * tokens, (s + 1) * tokens)
        values_ref[0:channels, here] = block
        keys_ref[here, :] = jnp.concatenate([block.astype(f32), unit], axis=0).T.astype(bf16)
    values_ref[channels : channels + 16, :] = (
        lax.broadcasted_iota(jnp.int32, (16, 2 * half * tokens), 0) == 0
    ).astype(bf16)
    own_ref[...] = jnp.zeros_like(own_ref)
    for c in range(CORES):
        block = jnp.where(core_ref[0] == c, near_ref[0], far_ref[0])
        for p in range(2):
            left = (CORES * p + c) * tokens
            own_ref[p * channels : (p + 1) * channels, left : left + tokens] = block


def attend_kernel(
    pack_ref,
    keys_ref,
    values_ref,
    own_ref,
    before_ref,
    shared_ref,
    attended_ref,
    outward_ref,
    queries_ref,
    scores_ref,
    top_ref,
):
    pairs = pack_ref.shape[0]
    heads = 2 * pairs
    channels, wide = before_ref.shape
    length = keys_ref.shape[0]

    own = own_ref[...]
    tails = pack_ref[:, 2 * channels : 2 * channels + 16, :]
    levels = dot(tails.reshape(pairs * 16, LANES), own)
    tails = tails.astype(f32)
    constants = jnp.concatenate(
        [tails[s, 0:1] for s in range(pairs)]
        + [jnp.sum(tails, axis=0), jnp.zeros((LANES - 16 - pairs, LANES), f32)],
        axis=0,
    ).T
    queries = dot(pack_ref[:, 0:channels, :].reshape(pairs * channels, LANES), own)
    first = lax.broadcasted_iota(jnp.int32, (16, wide), 0) == 0
    for s in range(pairs):
        outward_ref[:, s * LANES : (s + 1) * LANES] = pack_ref[s, channels : 2 * channels, :]
        for p in range(2):
            here = slice(p * wide, (p + 1) * wide)
            shift = constants[p * channels : (p + 1) * channels, s : s + 1]
            level = levels[16 * s + 1 : 16 * s + 2, here] + tails[s, 2:3, p * channels : p * channels + 1]
            queries_ref[2 * s + p, 0:channels, :] = (
                queries[s * channels : (s + 1) * channels, here] + shift
            ).astype(bf16)
            queries_ref[2 * s + p, channels : channels + 16, :] = jnp.where(first, level, 0.0).astype(bf16)
            queries_ref[2 * s + p, channels + 16 :, :] = jnp.zeros((LANES - channels - 16, wide), bf16)

    part = 256

    def start(slot, h):
        query = queries_ref[h]
        top = None
        for c in range(length // part):
            scores = dot(keys_ref[c * part : (c + 1) * part, :], query)
            scores_ref[slot, c * part : (c + 1) * part, :] = scores
            high = jnp.max(scores.reshape(part // 8, 8, wide), axis=0)
            top = high if top is None else jnp.maximum(top, high)
        top_ref[slot] = top

    def finish(slot, h):
        top = jnp.max(top_ref[slot], axis=0, keepdims=True)
        probs = jnp.exp2(scores_ref[slot] - top).astype(bf16)
        sums = dot(values_ref[...], probs)
        attended_ref[h] = (sums[0:channels] * (1.0 / sums[channels : channels + 1])).astype(bf16)

    start(0, 0)

    def body(i, carry):
        start(1, 2 * i + 1)
        finish(0, 2 * i)
        start(0, lax.rem(2 * i + 2, heads))
        finish(1, 2 * i + 1)
        return carry

    lax.fori_loop(0, pairs, body, 0, unroll=2)

    shared_ref[...] = (
        before_ref[...]
        + dot(outward_ref[...], attended_ref[...].reshape(heads * channels, wide))
        + constants[0:channels, pairs + 3 : pairs + 4]
    )


def finish_kernel(
    core_ref,
    chip_ref,
    mine_ref,
    other_ref,
    attended_ref,
    attended_far_ref,
    drawn_ref,
    fresh_ref,
    pieces_ref,
    *,
    steps_count,
):
    channels, tokens = drawn_ref.shape
    wide = CORES * tokens
    is_first = core_ref[0] == 0
    change = (mine_ref[:, 0:wide] + other_ref[:, 0:wide]) * (1.0 / steps_count)
    mine, other = mine_ref[:, wide:], other_ref[:, wide:]
    residual = change + jnp.concatenate(
        [jnp.where(is_first, mine, other), jnp.where(is_first, other, mine)], axis=1
    )
    own = jnp.where(is_first, change[:, 0:tokens], change[:, tokens:])
    fresh_ref[...] = (drawn_ref[...] - own).astype(bf16)
    squared = jnp.sum(jnp.sum(residual * residual, axis=1, keepdims=True), axis=0, keepdims=True)
    residual = residual.astype(bf16)
    padded = jnp.concatenate([residual, jnp.zeros((LANES - channels, wide), bf16)], axis=0)
    column_sums = dot_nt(jnp.ones((16, wide), bf16), padded)
    slot = lax.broadcasted_iota(jnp.int32, (16, LANES), 0)
    high = squared.astype(bf16).astype(f32)
    tail = jnp.where(slot == 0, column_sums, jnp.where(slot == 1, high, jnp.where(slot == 2, squared - high, 0.0)))
    tail = tail.astype(bf16)
    half = pieces_ref.shape[0] // 2
    for part, bits in ((attended_ref, 0), (attended_far_ref, 2 * half - 1)):
        product = dot_nt(residual, part[...].reshape(2 * half * channels, wide)).astype(bf16)
        for s in range(half):
            place = chip_ref[0] ^ (s ^ bits)
            pieces_ref[place, 0:channels, :] = product[:, s * LANES : (s + 1) * LANES]
            pieces_ref[place, channels : channels + 16, :] = tail


def gradient_kernel(pieces_ref, values_ref, offsets_ref, gain_ref, old_ref, out_ref, *, entries):
    total = pieces_ref[0].astype(f32)
    for s in range(1, pieces_ref.shape[0]):
        total += pieces_ref[s].astype(f32)
    channels = out_ref.shape[1]
    tail = total[channels : channels + 16]
    squared = tail[1:2, 0:1] + tail[2:3, 0:1]
    logp = -squared / (2.0 * noise_level * noise_level * entries)
    scale = gain_ref[0] * jnp.exp(logp - old_ref[0])
    column = jnp.concatenate([tail, jnp.zeros((LANES - 16, LANES), f32)], axis=0).T[0:channels, 0:1]
    product = total[0:channels]
    none = jnp.zeros((channels, LANES), f32)
    parts = []
    for h in range(2):
        values = values_ref[h * channels : (h + 1) * channels, :]
        padded = jnp.concatenate([values, none] if h == 0 else [none, values], axis=0)
        parts.append(dot(product, padded, HIGHEST) + column * offsets_ref[4 + h : 5 + h, :])
    gradient = (jnp.concatenate(parts, axis=1) * scale).astype(bf16)
    for i in range(out_ref.shape[0]):
        out_ref[i] = gradient


def total_kernel(parts_ref, gradient_ref, squares_ref):
    gradient = parts_ref[0].astype(f32)
    for i in range(1, parts_ref.shape[0]):
        gradient += parts_ref[i].astype(f32)
    gradient_ref[...] = gradient
    squares = jnp.sum(gradient * gradient, axis=0, keepdims=True)
    squares = squares[:, 0:LANES] + squares[:, LANES:]
    for s in range(squares_ref.shape[0]):
        squares_ref[s] = squares


def update_kernel(role_ref, gradient_ref, squares_ref, head_ref, fresh_ref, out_ref, *, entries):
    squares = squares_ref[0]
    for s in range(1, squares_ref.shape[0]):
        squares += squares_ref[s]
    mean_square = jnp.sum(squares, axis=1, keepdims=True) * (1.0 / entries)
    change = step_size * gradient_ref[...] * lax.rsqrt(mean_square + update_eps)
    fresh = fresh_ref[...]
    fresh = jnp.concatenate([fresh, jnp.zeros_like(fresh)], axis=1)
    out_ref[...] = jnp.where(role_ref[0] == 1, (head_ref[...].astype(f32) - change).astype(bf16), fresh)


def output_kernel(role_ref, mine_ref, other_ref, fresh_ref, head_ref):
    learner = role_ref[0] == 1
    mine, other = mine_ref[...], other_ref[...]
    head_ref[...] = jnp.where(learner, mine, other)
    fresh_ref[...] = jnp.where(learner, other, mine)[:, 0 : fresh_ref.shape[1]]


def call(kernel, outs, specs, scratch=(), flops=0, mib=32, place=VMEM):
    single = not isinstance(outs, (list, tuple))
    return pl.pallas_call(
        kernel,
        out_shape=outs,
        in_specs=specs,
        out_specs=place if single else [place] * len(outs),
        scratch_shapes=list(scratch),
        compiler_params=pltpu.CompilerParams(vmem_limit_bytes=mib * 1024 * 1024),
        cost_estimate=pl.CostEstimate(flops=flops, bytes_accessed=0, transcendentals=0),
    )


def shape(*dims, dtype=f32):
    return jax.ShapeDtypeStruct(dims, dtype)


def on_device(
    latents,
    next_latents,
    noise,
    advantage,
    old_logp,
    timesteps,
    embed_weight,
    modulation,
    qkv_weight,
    head_weight,
):
    core = (lax.axis_index("seq") % CORES).reshape(1)
    chip = (lax.axis_index("seq") // CORES).reshape(1)
    rollouts, blocks = lax.axis_size("dp"), lax.axis_size("seq")
    chips = blocks // CORES
    along = [[CORES * z + c for z in range(chips)] for c in range(CORES)]
    latent = latents[0, 0].T
    channels, tokens = latent.shape
    steps_count, _, width = modulation.shape
    rows, columns = qkv_weight.shape[2:]
    wide = CORES * tokens
    head = head_weight[0].T

    def across(value, axis, bits):
        return lax.ppermute(value, axis, [(i, i ^ bits) for i in range(lax.axis_size(axis))])

    steps = call(step_kernel, shape(rollouts, 1, LANES, dtype=jnp.int32), [SMEM], mib=1)(timesteps)
    steps = lax.all_to_all(steps, "dp", 0, 0)[:, 0, 0]
    place = lax.axis_index("dp").reshape(1)
    near, centered, ahead, drawn = call(
        token_kernel,
        [
            shape(channels, tokens, dtype=bf16),
            shape(channels, rows),
            shape(channels, tokens),
            shape(channels, tokens),
        ],
        [SMEM] + [VMEM] * 4,
        flops=10**9,
        mib=16,
    )(place, latent, next_latents[0].T, noise[0].T, embed_weight)

    near = jnp.stack([near, across(near, "seq", 14)])
    near = jnp.concatenate([near] + [across(near, "seq", bits) for bits in (2, 4, 6)], axis=0)
    far = across(near, "seq", 1)
    sums = call(
        partial_kernel,
        shape(steps_count, 6 * channels + 16, LANES, dtype=bf16),
        [SMEM] + [VMEM] * 3,
        [pltpu.VMEM((steps_count * (channels + 16), rows), bf16)],
        flops=3 * 10**9,
        mib=16,
    )(place, centered, modulation, qkv_weight[0])
    sums = call(
        choose_kernel, shape(rollouts, 6 * channels + 16, LANES, dtype=bf16), [SMEM, VMEM], mib=16
    )(steps, sums)

    sums = lax.all_to_all(sums, "dp", 0, 0)
    pack, values, offsets = call(
        functools.partial(absorb_kernel, factor=width**-0.5, logit=math.log2(math.e) / HD**0.5),
        [shape(1, 2 * channels + 16, LANES, dtype=bf16), shape(2 * channels, HD), shape(8, HD)],
        [VMEM] * 2,
    )(sums, head)
    pack = jnp.concatenate([pack] + [across(pack, "seq", bits) for bits in (2, 4, 6)], axis=0)
    pack_far = across(pack, "seq", 14)
    keys, spread, own = call(
        tokens_kernel,
        [
            shape(blocks * tokens, LANES, dtype=bf16),
            shape(channels + 16, blocks * tokens, dtype=bf16),
            shape(2 * channels, 2 * wide, dtype=bf16),
        ],
        [SMEM, VMEM, VMEM],
        flops=10**9,
    )(core, near, far)
    def attend(pack, before):
        count = pack.shape[0]
        return call(
            attend_kernel,
            [shape(channels, wide), shape(2 * count, channels, wide, dtype=bf16)],
            [VMEM] * 5,
            [
                pltpu.VMEM((channels, count * LANES), bf16),
                pltpu.VMEM((2 * count, LANES, wide), bf16),
                pltpu.VMEM((2, blocks * tokens, wide), f32),
                pltpu.VMEM((2, 8, wide), f32),
            ],
            flops=4 * 10**9,
        )(pack, keys, spread, own, before)

    shared, attended = attend(pack, jnp.zeros((channels, wide), f32))
    shared, attended_far = attend(pack_far, shared)
    shared = jnp.concatenate([shared, ahead], axis=1)
    other = across(shared, "seq", 1)
    fresh, pieces = call(
        functools.partial(finish_kernel, steps_count=steps_count),
        [shape(channels, tokens, dtype=bf16), shape(chips, channels + 16, LANES, dtype=bf16)],
        [SMEM, SMEM] + [VMEM] * 5,
    )(core, chip, shared, other, attended, attended_far, drawn)
    pieces = lax.all_to_all(pieces, "seq", 0, 0, axis_index_groups=along)
    parts = call(
        functools.partial(gradient_kernel, entries=tokens * blocks * channels),
        shape(rollouts, channels, columns, dtype=bf16),
        [VMEM, VMEM, VMEM, SMEM, SMEM],
    )(pieces, values, offsets, advantage, old_logp)
    parts = lax.all_to_all(parts, "dp", 0, 0)
    gradient, squares = call(
        total_kernel,
        [shape(channels, columns), shape(blocks, 1, LANES)],
        [VMEM],
    )(parts)
    squares = lax.all_to_all(squares, "seq", 0, 0)
    role = lax.axis_index("role").reshape(1)
    mine = call(
        functools.partial(update_kernel, entries=columns * blocks * channels),
        shape(channels, columns, dtype=bf16),
        [SMEM] + [VMEM] * 4,
    )(role, gradient, squares, head, fresh)
    other = lax.ppermute(mine, "role", [(0, 1), (1, 0)])
    fresh_out, head_out = call(
        output_kernel,
        [shape(channels, tokens, dtype=bf16), shape(channels, columns, dtype=bf16)],
        [SMEM, VMEM, VMEM],
    )(role, mine, other)
    return (fresh_out.T[None, None], head_out.T[None])


def solution(mesh):
    in_specs = (
        P("role", "dp", "seq", None),
        P("dp", "seq", None),
        P("dp", "seq", None),
        P("dp"),
        P("dp"),
        P("role", "dp"),
        P(),
        P(),
        P("role", None, "dp", "seq"),
        P("role", "seq", None),
    )
    out_specs = (P("role", "dp", "seq", None), P("role", "seq", None))
    return jax.shard_map(
        on_device, mesh=mesh, in_specs=in_specs, out_specs=out_specs, check_vma=False
    )
```

```python
import functools
import math

import jax
import jax.numpy as jnp
from jax import lax
from jax.experimental import pallas as pl
from jax.experimental.pallas import tpu as pltpu
from jax.sharding import PartitionSpec as P

HD = 128
LANES = 128
CORES = 2

noise_level = 0.8
step_size = 0.5
norm_eps = 1e-06
update_eps = 1e-06

bf16 = jnp.bfloat16
f32 = jnp.float32

VMEM = pl.BlockSpec(memory_space=pltpu.VMEM)
SMEM = pl.BlockSpec(memory_space=pltpu.SMEM)
HBM = pl.BlockSpec(memory_space=pltpu.HBM)


def dot(a, b, precision=None):
    return lax.dot_general(
        a, b, (((1,), (0,)), ((), ())), precision=precision, preferred_element_type=f32
    )


def dot_nt(a, b, precision=None):
    return lax.dot_general(
        a, b, (((1,), (1,)), ((), ())), precision=precision, preferred_element_type=f32
    )


HIGHEST = lax.Precision.HIGHEST


def token_kernel(place_ref, latent_ref, next_ref, noise_ref, embed_ref, tokens_ref, centered_ref, ahead_ref, drawn_ref):
    latent = latent_ref[...].astype(f32)
    ahead_ref[...] = next_ref[...].astype(f32) - latent
    drawn_ref[...] = latent + noise_level * noise_ref[...].astype(f32)
    embed = embed_ref[...]
    embedded = dot(latent.T.astype(bf16), embed).astype(bf16).astype(f32)
    width = embedded.shape[1]
    center = jnp.sum(embedded, axis=1, keepdims=True) * (1.0 / width)
    spread = jnp.sum((embedded - center) * (embedded - center), axis=1, keepdims=True) * (1.0 / width)
    tokens_ref[...] = (latent.T * lax.rsqrt(spread + norm_eps)).T.astype(bf16)
    mean = jnp.sum(embed.astype(f32), axis=1, keepdims=True) * (1.0 / width)
    rows = centered_ref.shape[1]
    start = pl.multiple_of(place_ref[0] * rows, LANES)
    centered_ref[...] = embed_ref[:, pl.ds(start, rows)].astype(f32) - mean


def partial_kernel(place_ref, centered_ref, modulation_ref, weight_ref, sums_ref, left_ref):
    channels, rows = centered_ref.shape
    steps = sums_ref.shape[0]
    block = channels + 16
    start = pl.multiple_of(place_ref[0] * rows, LANES)
    centered = centered_ref[...]
    row = lax.broadcasted_iota(jnp.int32, (16, rows), 0)
    for i in range(steps):
        shift = modulation_ref[i, 0:1, pl.ds(start, rows)]
        scale = modulation_ref[i, 1:2, pl.ds(start, rows)]
        high = shift.astype(bf16).astype(f32)
        tail = jnp.where(row == 0, high, jnp.where(row == 1, shift - high, 0.0))
        left_ref[i * block : i * block + channels, :] = (centered * (1.0 + scale)).astype(bf16)
        left_ref[i * block + channels : (i + 1) * block, :] = tail.astype(bf16)
    slot = lax.broadcasted_iota(jnp.int32, (16, LANES), 0)
    tails = [jnp.zeros((16, LANES), f32) for _ in range(steps)]
    for j in range(3):
        product = dot(left_ref[...], weight_ref[j])
        for i in range(steps):
            for h in range(2):
                c = 2 * j + h
                part = product[i * block : (i + 1) * block, h * HD : (h + 1) * HD]
                sums_ref[i, c * channels : (c + 1) * channels, :] = part[:channels].astype(bf16)
                offset = part[channels : channels + 1] + part[channels + 1 : channels + 2]
                high = offset.astype(bf16).astype(f32)
                tails[i] = jnp.where(slot == c, high, jnp.where(slot == c + 8, offset - high, tails[i]))
    for i in range(steps):
        sums_ref[i, 6 * channels : 6 * channels + 16, :] = tails[i].astype(bf16)


def step_kernel(step_ref, out_ref):
    out_ref[...] = jnp.broadcast_to(step_ref[0, 0], out_ref.shape)


def choose_kernel(steps_ref, sums_ref, out_ref):
    for i in range(out_ref.shape[0]):
        out_ref[i] = sums_ref[steps_ref[i]]


def absorb_kernel(sums_ref, head_ref, pack_ref, values_ref, offsets_ref, *, factor, logit):
    channels = head_ref.shape[0]
    total = sums_ref[0].astype(f32)
    for i in range(1, sums_ref.shape[0]):
        total += sums_ref[i].astype(f32)
    total = total * factor
    blocks = [total[c * channels : (c + 1) * channels] for c in range(6)]
    offsets = total[6 * channels : 6 * channels + 8] + total[6 * channels + 8 : 6 * channels + 16]
    queries, keys, values = blocks[0:2], blocks[2:4], blocks[4:6]
    none = jnp.zeros((channels, LANES), f32)

    def beside(parts):
        return jnp.concatenate([parts[0], none], axis=0), jnp.concatenate([none, parts[1]], axis=0)

    heads = [head_ref[:, h * HD : (h + 1) * HD].astype(f32) for h in range(2)]
    query_pads, key_pads, value_pads = beside(queries), beside(keys), beside(values)
    bilinear = sum(dot_nt(keys[h], query_pads[h], HIGHEST) for h in range(2)) * logit
    outward = sum(dot_nt(heads[h], value_pads[h], HIGHEST) for h in range(2))

    slot = lax.broadcasted_iota(jnp.int32, (8, LANES), 0)
    lane = lax.broadcasted_iota(jnp.int32, (8, LANES), 1)

    def pick(array, c):
        return jnp.sum(jnp.where(slot == c, array, 0.0), axis=0, keepdims=True)

    by_keys = [dot_nt(offsets, key_pads[h], HIGHEST) * logit for h in range(2)]
    by_queries = [dot_nt(offsets, query_pads[h], HIGHEST) * logit for h in range(2)]
    by_heads = [dot_nt(offsets, jnp.concatenate([heads[h], none], axis=0), HIGHEST) for h in range(2)]
    query_constant = pick(by_keys[0], 0) + pick(by_keys[1], 1)
    key_constant = pick(by_queries[0], 2) + pick(by_queries[1], 3)
    both = [
        jnp.sum(pick(offsets, h) * pick(offsets, 2 + h), axis=1, keepdims=True) * logit for h in range(2)
    ]
    outward_constant = pick(by_heads[0], 4) + pick(by_heads[1], 5)
    tail = jnp.where(slot == 0, query_constant, 0.0)
    tail = jnp.where(slot == 1, key_constant, tail)
    tail = jnp.where(slot == 2, jnp.where(lane < channels, both[0], both[1]), tail)
    tail = jnp.where(slot == 3, outward_constant, tail)
    pack_ref[0] = jnp.concatenate([bilinear, outward, tail, jnp.zeros_like(tail)], axis=0).astype(bf16)
    values_ref[0:channels, :] = values[0]
    values_ref[channels : 2 * channels, :] = values[1]
    offsets_ref[...] = offsets


def tokens_kernel(core_ref, near_ref, far_ref, keys_ref, values_ref, own_ref):
    half, channels, tokens = near_ref.shape
    unit = (lax.broadcasted_iota(jnp.int32, (LANES - channels, tokens), 0) == 0).astype(f32)
    for s in range(2 * half):
        block = near_ref[s] if s < half else far_ref[s - half]
        here = slice(s * tokens, (s + 1) * tokens)
        values_ref[0:channels, here] = block
        keys_ref[here, :] = jnp.concatenate([block.astype(f32), unit], axis=0).T.astype(bf16)
    values_ref[channels : channels + 16, :] = (
        lax.broadcasted_iota(jnp.int32, (16, 2 * half * tokens), 0) == 0
    ).astype(bf16)
    own_ref[...] = jnp.zeros_like(own_ref)
    for c in range(CORES):
        block = jnp.where(core_ref[0] == c, near_ref[0], far_ref[0])
        for p in range(2):
            left = (CORES * p + c) * tokens
            own_ref[p * channels : (p + 1) * channels, left : left + tokens] = block


def attend_kernel(
    pack_ref,
    keys_ref,
    values_ref,
    own_ref,
    before_ref,
    shared_ref,
    attended_ref,
    outward_ref,
    queries_ref,
    scores_ref,
    top_ref,
):
    pairs = pack_ref.shape[0]
    heads = 2 * pairs
    channels, wide = before_ref.shape
    length = keys_ref.shape[0]

    own = own_ref[...]
    tails = pack_ref[:, 2 * channels : 2 * channels + 16, :]
    levels = dot(tails.reshape(pairs * 16, LANES), own)
    tails = tails.astype(f32)
    constants = jnp.concatenate(
        [tails[s, 0:1] for s in range(pairs)]
        + [jnp.sum(tails, axis=0), jnp.zeros((LANES - 16 - pairs, LANES), f32)],
        axis=0,
    ).T
    queries = dot(pack_ref[:, 0:channels, :].reshape(pairs * channels, LANES), own)
    first = lax.broadcasted_iota(jnp.int32, (16, wide), 0) == 0
    for s in range(pairs):
        outward_ref[:, s * LANES : (s + 1) * LANES] = pack_ref[s, channels : 2 * channels, :]
        for p in range(2):
            here = slice(p * wide, (p + 1) * wide)
            shift = constants[p * channels : (p + 1) * channels, s : s + 1]
            level = levels[16 * s + 1 : 16 * s + 2, here] + tails[s, 2:3, p * channels : p * channels + 1]
            queries_ref[2 * s + p, 0:channels, :] = (
                queries[s * channels : (s + 1) * channels, here] + shift
            ).astype(bf16)
            queries_ref[2 * s + p, channels : channels + 16, :] = jnp.where(first, level, 0.0).astype(bf16)
            queries_ref[2 * s + p, channels + 16 :, :] = jnp.zeros((LANES - channels - 16, wide), bf16)

    part = 256

    def start(slot, h):
        query = queries_ref[h]
        top = None
        for c in range(length // part):
            scores = dot(keys_ref[c * part : (c + 1) * part, :], query)
            scores_ref[slot, c * part : (c + 1) * part, :] = scores
            high = jnp.max(scores.reshape(part // 8, 8, wide), axis=0)
            top = high if top is None else jnp.maximum(top, high)
        top_ref[slot] = top

    def finish(slot, h):
        top = jnp.max(top_ref[slot], axis=0, keepdims=True)
        probs = jnp.exp2(scores_ref[slot] - top).astype(bf16)
        sums = dot(values_ref[...], probs)
        attended_ref[h] = (sums[0:channels] * (1.0 / sums[channels : channels + 1])).astype(bf16)

    start(0, 0)

    def body(i, carry):
        start(1, 2 * i + 1)
        finish(0, 2 * i)
        start(0, lax.rem(2 * i + 2, heads))
        finish(1, 2 * i + 1)
        return carry

    lax.fori_loop(0, pairs, body, 0, unroll=2)

    shared_ref[...] = (
        before_ref[...]
        + dot(outward_ref[...], attended_ref[...].reshape(heads * channels, wide))
        + constants[0:channels, pairs + 3 : pairs + 4]
    )


def finish_kernel(
    core_ref,
    chip_ref,
    mine_ref,
    other_ref,
    attended_ref,
    attended_far_ref,
    drawn_ref,
    fresh_ref,
    pieces_ref,
    *,
    steps_count,
):
    channels, tokens = drawn_ref.shape
    wide = CORES * tokens
    is_first = core_ref[0] == 0
    change = (mine_ref[:, 0:wide] + other_ref[:, 0:wide]) * (1.0 / steps_count)
    mine, other = mine_ref[:, wide:], other_ref[:, wide:]
    residual = change + jnp.concatenate(
        [jnp.where(is_first, mine, other), jnp.where(is_first, other, mine)], axis=1
    )
    own = jnp.where(is_first, change[:, 0:tokens], change[:, tokens:])
    fresh_ref[...] = (drawn_ref[...] - own).astype(bf16)
    squared = jnp.sum(jnp.sum(residual * residual, axis=1, keepdims=True), axis=0, keepdims=True)
    residual = residual.astype(bf16)
    padded = jnp.concatenate([residual, jnp.zeros((LANES - channels, wide), bf16)], axis=0)
    column_sums = dot_nt(jnp.ones((16, wide), bf16), padded)
    slot = lax.broadcasted_iota(jnp.int32, (16, LANES), 0)
    high = squared.astype(bf16).astype(f32)
    tail = jnp.where(slot == 0, column_sums, jnp.where(slot == 1, high, jnp.where(slot == 2, squared - high, 0.0)))
    tail = tail.astype(bf16)
    half = pieces_ref.shape[0] // 2
    for part, bits in ((attended_ref, 0), (attended_far_ref, 2 * half - 1)):
        product = dot_nt(residual, part[...].reshape(2 * half * channels, wide)).astype(bf16)
        for s in range(half):
            place = chip_ref[0] ^ (s ^ bits)
            pieces_ref[place, 0:channels, :] = product[:, s * LANES : (s + 1) * LANES]
            pieces_ref[place, channels : channels + 16, :] = tail


def gradient_kernel(pieces_ref, values_ref, offsets_ref, gain_ref, old_ref, out_ref, *, entries):
    total = pieces_ref[0].astype(f32)
    for s in range(1, pieces_ref.shape[0]):
        total += pieces_ref[s].astype(f32)
    channels = out_ref.shape[1]
    tail = total[channels : channels + 16]
    squared = tail[1:2, 0:1] + tail[2:3, 0:1]
    logp = -squared / (2.0 * noise_level * noise_level * entries)
    scale = gain_ref[0] * jnp.exp(logp - old_ref[0])
    column = jnp.concatenate([tail, jnp.zeros((LANES - 16, LANES), f32)], axis=0).T[0:channels, 0:1]
    product = total[0:channels]
    none = jnp.zeros((channels, LANES), f32)
    parts = []
    for h in range(2):
        values = values_ref[h * channels : (h + 1) * channels, :]
        padded = jnp.concatenate([values, none] if h == 0 else [none, values], axis=0)
        parts.append(dot(product, padded, HIGHEST) + column * offsets_ref[4 + h : 5 + h, :])
    gradient = (jnp.concatenate(parts, axis=1) * scale).astype(bf16)
    for i in range(out_ref.shape[0]):
        out_ref[i] = gradient


def total_kernel(parts_ref, gradient_ref, squares_ref):
    gradient = parts_ref[0].astype(f32)
    for i in range(1, parts_ref.shape[0]):
        gradient += parts_ref[i].astype(f32)
    gradient_ref[...] = gradient
    squares = jnp.sum(gradient * gradient, axis=0, keepdims=True)
    squares = squares[:, 0:LANES] + squares[:, LANES:]
    for s in range(squares_ref.shape[0]):
        squares_ref[s] = squares


def update_kernel(role_ref, gradient_ref, squares_ref, head_ref, fresh_ref, out_ref, *, entries):
    squares = squares_ref[0]
    for s in range(1, squares_ref.shape[0]):
        squares += squares_ref[s]
    mean_square = jnp.sum(squares, axis=1, keepdims=True) * (1.0 / entries)
    change = step_size * gradient_ref[...] * lax.rsqrt(mean_square + update_eps)
    fresh = fresh_ref[...]
    fresh = jnp.concatenate([fresh, jnp.zeros_like(fresh)], axis=1)
    out_ref[...] = jnp.where(role_ref[0] == 1, (head_ref[...].astype(f32) - change).astype(bf16), fresh)


def output_kernel(role_ref, mine_ref, other_ref, fresh_ref, head_ref):
    learner = role_ref[0] == 1
    mine, other = mine_ref[...], other_ref[...]
    head_ref[...] = jnp.where(learner, mine, other)
    fresh_ref[...] = jnp.where(learner, other, mine)[:, 0 : fresh_ref.shape[1]]


def call(kernel, outs, specs, scratch=(), flops=0, mib=32, place=VMEM):
    single = not isinstance(outs, (list, tuple))
    return pl.pallas_call(
        kernel,
        out_shape=outs,
        in_specs=specs,
        out_specs=place if single else [place] * len(outs),
        scratch_shapes=list(scratch),
        compiler_params=pltpu.CompilerParams(vmem_limit_bytes=mib * 1024 * 1024),
        cost_estimate=pl.CostEstimate(flops=flops, bytes_accessed=0, transcendentals=0),
    )


def shape(*dims, dtype=f32):
    return jax.ShapeDtypeStruct(dims, dtype)


def on_device(
    latents,
    next_latents,
    noise,
    advantage,
    old_logp,
    timesteps,
    embed_weight,
    modulation,
    qkv_weight,
    head_weight,
):
    core = (lax.axis_index("seq") % CORES).reshape(1)
    chip = (lax.axis_index("seq") // CORES).reshape(1)
    rollouts, blocks = lax.axis_size("dp"), lax.axis_size("seq")
    chips = blocks // CORES
    along = [[CORES * z + c for z in range(chips)] for c in range(CORES)]
    latent = latents[0, 0].T
    channels, tokens = latent.shape
    steps_count, _, width = modulation.shape
    rows, columns = qkv_weight.shape[2:]
    wide = CORES * tokens
    head = head_weight[0].T

    def across(value, axis, bits):
        return lax.ppermute(value, axis, [(i, i ^ bits) for i in range(lax.axis_size(axis))])

    steps = call(step_kernel, shape(rollouts, 1, LANES, dtype=jnp.int32), [SMEM], mib=1)(timesteps)
    steps = lax.all_to_all(steps, "dp", 0, 0)[:, 0, 0]
    place = lax.axis_index("dp").reshape(1)
    near, centered, ahead, drawn = call(
        token_kernel,
        [
            shape(channels, tokens, dtype=bf16),
            shape(channels, rows),
            shape(channels, tokens),
            shape(channels, tokens),
        ],
        [SMEM] + [VMEM] * 4,
        flops=10**9,
        mib=16,
    )(place, latent, next_latents[0].T, noise[0].T, embed_weight)

    near = jnp.stack([near, across(near, "seq", 14)])
    near = jnp.concatenate([near] + [across(near, "seq", bits) for bits in (2, 4, 6)], axis=0)
    sums = call(
        partial_kernel,
        shape(steps_count, 6 * channels + 16, LANES, dtype=bf16),
        [SMEM] + [VMEM] * 3,
        [pltpu.VMEM((steps_count * (channels + 16), rows), bf16)],
        flops=3 * 10**9,
        mib=16,
    )(place, centered, modulation, qkv_weight[0])
    sums = call(
        choose_kernel, shape(rollouts, 6 * channels + 16, LANES, dtype=bf16), [SMEM, VMEM], mib=16
    )(steps, sums)

    sums = lax.all_to_all(sums, "dp", 0, 0)
    sums, near = lax.optimization_barrier((sums, near))
    far = across(near, "seq", 1)
    pack, values, offsets = call(
        functools.partial(absorb_kernel, factor=width**-0.5, logit=math.log2(math.e) / HD**0.5),
        [shape(1, 2 * channels + 16, LANES, dtype=bf16), shape(2 * channels, HD), shape(8, HD)],
        [VMEM] * 2,
    )(sums, head)
    pack = jnp.concatenate([pack] + [across(pack, "seq", bits) for bits in (2, 4, 6)], axis=0)
    pack_far = across(pack, "seq", 14)
    keys, spread, own = call(
        tokens_kernel,
        [
            shape(blocks * tokens, LANES, dtype=bf16),
            shape(channels + 16, blocks * tokens, dtype=bf16),
            shape(2 * channels, 2 * wide, dtype=bf16),
        ],
        [SMEM, VMEM, VMEM],
        flops=10**9,
    )(core, near, far)
    def attend(pack, before):
        count = pack.shape[0]
        return call(
            attend_kernel,
            [shape(channels, wide), shape(2 * count, channels, wide, dtype=bf16)],
            [VMEM] * 5,
            [
                pltpu.VMEM((channels, count * LANES), bf16),
                pltpu.VMEM((2 * count, LANES, wide), bf16),
                pltpu.VMEM((2, blocks * tokens, wide), f32),
                pltpu.VMEM((2, 8, wide), f32),
            ],
            flops=4 * 10**9,
        )(pack, keys, spread, own, before)

    shared, attended = attend(pack, jnp.zeros((channels, wide), f32))
    shared, attended_far = attend(pack_far, shared)
    shared = jnp.concatenate([shared, ahead], axis=1)
    other = across(shared, "seq", 1)
    fresh, pieces = call(
        functools.partial(finish_kernel, steps_count=steps_count),
        [shape(channels, tokens, dtype=bf16), shape(chips, channels + 16, LANES, dtype=bf16)],
        [SMEM, SMEM] + [VMEM] * 5,
    )(core, chip, shared, other, attended, attended_far, drawn)
    pieces = lax.all_to_all(pieces, "seq", 0, 0, axis_index_groups=along)
    parts = call(
        functools.partial(gradient_kernel, entries=tokens * blocks * channels),
        shape(rollouts, channels, columns, dtype=bf16),
        [VMEM, VMEM, VMEM, SMEM, SMEM],
    )(pieces, values, offsets, advantage, old_logp)
    parts = lax.all_to_all(parts, "dp", 0, 0, axis_index_groups=[list(reversed(range(rollouts)))])
    gradient, squares = call(
        total_kernel,
        [shape(channels, columns), shape(blocks, 1, LANES)],
        [VMEM],
    )(parts)
    squares = lax.all_to_all(squares, "seq", 0, 0, axis_index_groups=[[(i + blocks // 2) % blocks for i in range(blocks)]])
    role = lax.axis_index("role").reshape(1)
    mine = call(
        functools.partial(update_kernel, entries=columns * blocks * channels),
        shape(channels, columns, dtype=bf16),
        [SMEM] + [VMEM] * 4,
    )(role, gradient, squares, head, fresh)
    other = lax.ppermute(mine, "role", [(0, 1), (1, 0)])
    fresh_out, head_out = call(
        output_kernel,
        [shape(channels, tokens, dtype=bf16), shape(channels, columns, dtype=bf16)],
        [SMEM, VMEM, VMEM],
    )(role, mine, other)
    return (fresh_out.T[None, None], head_out.T[None])


def solution(mesh):
    in_specs = (
        P("role", "dp", "seq", None),
        P("dp", "seq", None),
        P("dp", "seq", None),
        P("dp"),
        P("dp"),
        P("role", "dp"),
        P(),
        P(),
        P("role", None, "dp", "seq"),
        P("role", "seq", None),
    )
    out_specs = (P("role", "dp", "seq", None), P("role", "seq", None))
    return jax.shard_map(
        on_device, mesh=mesh, in_specs=in_specs, out_specs=out_specs, check_vma=False
    )
```

```python
import functools
import math

import jax
import jax.numpy as jnp
from jax import lax
from jax.experimental import pallas as pl
from jax.experimental.pallas import tpu as pltpu
from jax.sharding import PartitionSpec as P

HD = 128
LANES = 128
CORES = 2

noise_level = 0.8
step_size = 0.5
norm_eps = 1e-06
update_eps = 1e-06

bf16 = jnp.bfloat16
f32 = jnp.float32

VMEM = pl.BlockSpec(memory_space=pltpu.VMEM)
SMEM = pl.BlockSpec(memory_space=pltpu.SMEM)
HBM = pl.BlockSpec(memory_space=pltpu.HBM)


def dot(a, b, precision=None):
    return lax.dot_general(
        a, b, (((1,), (0,)), ((), ())), precision=precision, preferred_element_type=f32
    )


def dot_nt(a, b, precision=None):
    return lax.dot_general(
        a, b, (((1,), (1,)), ((), ())), precision=precision, preferred_element_type=f32
    )


HIGHEST = lax.Precision.HIGHEST


def token_kernel(place_ref, latent_ref, next_ref, noise_ref, embed_ref, tokens_ref, centered_ref, ahead_ref, drawn_ref):
    latent = latent_ref[...].astype(f32)
    ahead_ref[...] = next_ref[...].astype(f32) - latent
    drawn_ref[...] = latent + noise_level * noise_ref[...].astype(f32)
    embed = embed_ref[...]
    embedded = dot(latent.T.astype(bf16), embed).astype(bf16).astype(f32)
    width = embedded.shape[1]
    center = jnp.sum(embedded, axis=1, keepdims=True) * (1.0 / width)
    spread = jnp.sum((embedded - center) * (embedded - center), axis=1, keepdims=True) * (1.0 / width)
    tokens_ref[...] = (latent.T * lax.rsqrt(spread + norm_eps)).T.astype(bf16)
    mean = jnp.sum(embed.astype(f32), axis=1, keepdims=True) * (1.0 / width)
    rows = centered_ref.shape[1]
    start = pl.multiple_of(place_ref[0] * rows, LANES)
    centered_ref[...] = embed_ref[:, pl.ds(start, rows)].astype(f32) - mean


def partial_kernel(place_ref, centered_ref, modulation_ref, weight_ref, sums_ref, left_ref):
    channels, rows = centered_ref.shape
    steps = sums_ref.shape[0]
    block = channels + 16
    start = pl.multiple_of(place_ref[0] * rows, LANES)
    centered = centered_ref[...]
    row = lax.broadcasted_iota(jnp.int32, (16, rows), 0)
    for i in range(steps):
        shift = modulation_ref[i, 0:1, pl.ds(start, rows)]
        scale = modulation_ref[i, 1:2, pl.ds(start, rows)]
        high = shift.astype(bf16).astype(f32)
        tail = jnp.where(row == 0, high, jnp.where(row == 1, shift - high, 0.0))
        left_ref[i * block : i * block + channels, :] = (centered * (1.0 + scale)).astype(bf16)
        left_ref[i * block + channels : (i + 1) * block, :] = tail.astype(bf16)
    slot = lax.broadcasted_iota(jnp.int32, (16, LANES), 0)
    tails = [jnp.zeros((16, LANES), f32) for _ in range(steps)]
    for j in range(3):
        product = dot(left_ref[...], weight_ref[j])
        for i in range(steps):
            for h in range(2):
                c = 2 * j + h
                part = product[i * block : (i + 1) * block, h * HD : (h + 1) * HD]
                sums_ref[i, c * channels : (c + 1) * channels, :] = part[:channels].astype(bf16)
                offset = part[channels : channels + 1] + part[channels + 1 : channels + 2]
                high = offset.astype(bf16).astype(f32)
                tails[i] = jnp.where(slot == c, high, jnp.where(slot == c + 8, offset - high, tails[i]))
    for i in range(steps):
        sums_ref[i, 6 * channels : 6 * channels + 16, :] = tails[i].astype(bf16)


def step_kernel(step_ref, out_ref):
    out_ref[...] = jnp.broadcast_to(step_ref[0, 0], out_ref.shape)


def choose_kernel(steps_ref, sums_ref, out_ref):
    for i in range(out_ref.shape[0]):
        out_ref[i] = sums_ref[steps_ref[i]]


def absorb_kernel(sums_ref, head_ref, pack_ref, values_ref, offsets_ref, *, factor, logit):
    channels = head_ref.shape[0]
    total = sums_ref[0].astype(f32)
    for i in range(1, sums_ref.shape[0]):
        total += sums_ref[i].astype(f32)
    total = total * factor
    blocks = [total[c * channels : (c + 1) * channels] for c in range(6)]
    offsets = total[6 * channels : 6 * channels + 8] + total[6 * channels + 8 : 6 * channels + 16]
    queries, keys, values = blocks[0:2], blocks[2:4], blocks[4:6]
    none = jnp.zeros((channels, LANES), f32)

    def beside(parts):
        return jnp.concatenate([parts[0], none], axis=0), jnp.concatenate([none, parts[1]], axis=0)

    heads = [head_ref[:, h * HD : (h + 1) * HD].astype(f32) for h in range(2)]
    query_pads, key_pads, value_pads = beside(queries), beside(keys), beside(values)
    bilinear = sum(dot_nt(keys[h], query_pads[h], HIGHEST) for h in range(2)) * logit
    outward = sum(dot_nt(heads[h], value_pads[h], HIGHEST) for h in range(2))

    slot = lax.broadcasted_iota(jnp.int32, (8, LANES), 0)
    lane = lax.broadcasted_iota(jnp.int32, (8, LANES), 1)

    def pick(array, c):
        return jnp.sum(jnp.where(slot == c, array, 0.0), axis=0, keepdims=True)

    by_keys = [dot_nt(offsets, key_pads[h], HIGHEST) * logit for h in range(2)]
    by_queries = [dot_nt(offsets, query_pads[h], HIGHEST) * logit for h in range(2)]
    by_heads = [dot_nt(offsets, jnp.concatenate([heads[h], none], axis=0), HIGHEST) for h in range(2)]
    query_constant = pick(by_keys[0], 0) + pick(by_keys[1], 1)
    key_constant = pick(by_queries[0], 2) + pick(by_queries[1], 3)
    both = [
        jnp.sum(pick(offsets, h) * pick(offsets, 2 + h), axis=1, keepdims=True) * logit for h in range(2)
    ]
    outward_constant = pick(by_heads[0], 4) + pick(by_heads[1], 5)
    tail = jnp.where(slot == 0, query_constant, 0.0)
    tail = jnp.where(slot == 1, key_constant, tail)
    tail = jnp.where(slot == 2, jnp.where(lane < channels, both[0], both[1]), tail)
    tail = jnp.where(slot == 3, outward_constant, tail)
    pack_ref[0] = jnp.concatenate([bilinear, outward, tail, jnp.zeros_like(tail)], axis=0).astype(bf16)
    values_ref[0:channels, :] = values[0]
    values_ref[channels : 2 * channels, :] = values[1]
    offsets_ref[...] = offsets


def tokens_kernel(core_ref, near_ref, far_ref, keys_ref, values_ref, own_ref):
    half, channels, tokens = near_ref.shape
    unit = (lax.broadcasted_iota(jnp.int32, (LANES - channels, tokens), 0) == 0).astype(f32)
    for s in range(2 * half):
        block = near_ref[s] if s < half else far_ref[s - half]
        here = slice(s * tokens, (s + 1) * tokens)
        values_ref[0:channels, here] = block
        keys_ref[here, :] = jnp.concatenate([block.astype(f32), unit], axis=0).T.astype(bf16)
    values_ref[channels : channels + 16, :] = (
        lax.broadcasted_iota(jnp.int32, (16, 2 * half * tokens), 0) == 0
    ).astype(bf16)
    own_ref[...] = jnp.zeros_like(own_ref)
    for c in range(CORES):
        block = jnp.where(core_ref[0] == c, near_ref[0], far_ref[0])
        for p in range(2):
            left = (CORES * p + c) * tokens
            own_ref[p * channels : (p + 1) * channels, left : left + tokens] = block


def attend_kernel(
    pack_ref,
    keys_ref,
    values_ref,
    own_ref,
    before_ref,
    shared_ref,
    attended_ref,
    outward_ref,
    queries_ref,
    scores_ref,
    top_ref,
):
    pairs = pack_ref.shape[0]
    heads = 2 * pairs
    channels, wide = before_ref.shape
    length = keys_ref.shape[0]

    own = own_ref[...]
    tails = pack_ref[:, 2 * channels : 2 * channels + 16, :]
    levels = dot(tails.reshape(pairs * 16, LANES), own)
    tails = tails.astype(f32)
    constants = jnp.concatenate(
        [tails[s, 0:1] for s in range(pairs)]
        + [jnp.sum(tails, axis=0), jnp.zeros((LANES - 16 - pairs, LANES), f32)],
        axis=0,
    ).T
    queries = dot(pack_ref[:, 0:channels, :].reshape(pairs * channels, LANES), own)
    first = lax.broadcasted_iota(jnp.int32, (16, wide), 0) == 0
    for s in range(pairs):
        outward_ref[:, s * LANES : (s + 1) * LANES] = pack_ref[s, channels : 2 * channels, :]
        for p in range(2):
            here = slice(p * wide, (p + 1) * wide)
            shift = constants[p * channels : (p + 1) * channels, s : s + 1]
            level = levels[16 * s + 1 : 16 * s + 2, here] + tails[s, 2:3, p * channels : p * channels + 1]
            queries_ref[2 * s + p, 0:channels, :] = (
                queries[s * channels : (s + 1) * channels, here] + shift
            ).astype(bf16)
            queries_ref[2 * s + p, channels : channels + 16, :] = jnp.where(first, level, 0.0).astype(bf16)
            queries_ref[2 * s + p, channels + 16 :, :] = jnp.zeros((LANES - channels - 16, wide), bf16)

    part = 256

    def start(slot, h):
        query = queries_ref[h]
        top = None
        for c in range(length // part):
            scores = dot(keys_ref[c * part : (c + 1) * part, :], query)
            scores_ref[slot, c * part : (c + 1) * part, :] = scores
            high = jnp.max(scores.reshape(part // 8, 8, wide), axis=0)
            top = high if top is None else jnp.maximum(top, high)
        top_ref[slot] = top

    def finish(slot, h):
        top = jnp.max(top_ref[slot], axis=0, keepdims=True)
        probs = jnp.exp2(scores_ref[slot] - top).astype(bf16)
        sums = dot(values_ref[...], probs)
        attended_ref[h] = (sums[0:channels] * (1.0 / sums[channels : channels + 1])).astype(bf16)

    start(0, 0)

    def body(i, carry):
        start(1, 2 * i + 1)
        finish(0, 2 * i)
        start(0, lax.rem(2 * i + 2, heads))
        finish(1, 2 * i + 1)
        return carry

    lax.fori_loop(0, pairs, body, 0, unroll=2)

    shared_ref[...] = (
        before_ref[...]
        + dot(outward_ref[...], attended_ref[...].reshape(heads * channels, wide))
        + constants[0:channels, pairs + 3 : pairs + 4]
    )


def finish_kernel(
    core_ref,
    chip_ref,
    mine_ref,
    other_ref,
    attended_ref,
    attended_far_ref,
    drawn_ref,
    fresh_ref,
    pieces_ref,
    *,
    steps_count,
):
    channels, tokens = drawn_ref.shape
    wide = CORES * tokens
    is_first = core_ref[0] == 0
    change = (mine_ref[:, 0:wide] + other_ref[:, 0:wide]) * (1.0 / steps_count)
    mine, other = mine_ref[:, wide:], other_ref[:, wide:]
    residual = change + jnp.concatenate(
        [jnp.where(is_first, mine, other), jnp.where(is_first, other, mine)], axis=1
    )
    own = jnp.where(is_first, change[:, 0:tokens], change[:, tokens:])
    fresh_ref[...] = (drawn_ref[...] - own).astype(bf16)
    squared = jnp.sum(jnp.sum(residual * residual, axis=1, keepdims=True), axis=0, keepdims=True)
    residual = residual.astype(bf16)
    padded = jnp.concatenate([residual, jnp.zeros((LANES - channels, wide), bf16)], axis=0)
    column_sums = dot_nt(jnp.ones((16, wide), bf16), padded)
    slot = lax.broadcasted_iota(jnp.int32, (16, LANES), 0)
    high = squared.astype(bf16).astype(f32)
    tail = jnp.where(slot == 0, column_sums, jnp.where(slot == 1, high, jnp.where(slot == 2, squared - high, 0.0)))
    tail = tail.astype(bf16)
    half = pieces_ref.shape[0] // 2
    for part, bits in ((attended_ref, 0), (attended_far_ref, 2 * half - 1)):
        product = dot_nt(residual, part[...].reshape(2 * half * channels, wide)).astype(bf16)
        for s in range(half):
            place = chip_ref[0] ^ (s ^ bits ^ (2 * half - 1))
            pieces_ref[place, 0:channels, :] = product[:, s * LANES : (s + 1) * LANES]
            pieces_ref[place, channels : channels + 16, :] = tail


def gradient_kernel(pieces_ref, values_ref, offsets_ref, gain_ref, old_ref, out_ref, *, entries):
    total = pieces_ref[0].astype(f32)
    for s in range(1, pieces_ref.shape[0]):
        total += pieces_ref[s].astype(f32)
    channels = out_ref.shape[1]
    tail = total[channels : channels + 16]
    squared = tail[1:2, 0:1] + tail[2:3, 0:1]
    logp = -squared / (2.0 * noise_level * noise_level * entries)
    scale = gain_ref[0] * jnp.exp(logp - old_ref[0])
    column = jnp.concatenate([tail, jnp.zeros((LANES - 16, LANES), f32)], axis=0).T[0:channels, 0:1]
    product = total[0:channels]
    none = jnp.zeros((channels, LANES), f32)
    parts = []
    for h in range(2):
        values = values_ref[h * channels : (h + 1) * channels, :]
        padded = jnp.concatenate([values, none] if h == 0 else [none, values], axis=0)
        parts.append(dot(product, padded, HIGHEST) + column * offsets_ref[4 + h : 5 + h, :])
    gradient = (jnp.concatenate(parts, axis=1) * scale).astype(bf16)
    for i in range(out_ref.shape[0]):
        out_ref[i] = gradient


def total_kernel(parts_ref, gradient_ref, squares_ref):
    gradient = parts_ref[0].astype(f32)
    for i in range(1, parts_ref.shape[0]):
        gradient += parts_ref[i].astype(f32)
    gradient_ref[...] = gradient
    squares = jnp.sum(gradient * gradient, axis=0, keepdims=True)
    squares = squares[:, 0:LANES] + squares[:, LANES:]
    for s in range(squares_ref.shape[0]):
        squares_ref[s] = squares


def update_kernel(role_ref, gradient_ref, squares_ref, head_ref, fresh_ref, out_ref, *, entries):
    squares = squares_ref[0]
    for s in range(1, squares_ref.shape[0]):
        squares += squares_ref[s]
    mean_square = jnp.sum(squares, axis=1, keepdims=True) * (1.0 / entries)
    change = step_size * gradient_ref[...] * lax.rsqrt(mean_square + update_eps)
    fresh = fresh_ref[...]
    fresh = jnp.concatenate([fresh, jnp.zeros_like(fresh)], axis=1)
    out_ref[...] = jnp.where(role_ref[0] == 1, (head_ref[...].astype(f32) - change).astype(bf16), fresh)


def output_kernel(role_ref, mine_ref, other_ref, fresh_ref, head_ref):
    learner = role_ref[0] == 1
    mine, other = mine_ref[...], other_ref[...]
    head_ref[...] = jnp.where(learner, mine, other)
    fresh_ref[...] = jnp.where(learner, other, mine)[:, 0 : fresh_ref.shape[1]]


def call(kernel, outs, specs, scratch=(), flops=0, mib=32, place=VMEM):
    single = not isinstance(outs, (list, tuple))
    return pl.pallas_call(
        kernel,
        out_shape=outs,
        in_specs=specs,
        out_specs=place if single else [place] * len(outs),
        scratch_shapes=list(scratch),
        compiler_params=pltpu.CompilerParams(vmem_limit_bytes=mib * 1024 * 1024),
        cost_estimate=pl.CostEstimate(flops=flops, bytes_accessed=0, transcendentals=0),
    )


def shape(*dims, dtype=f32):
    return jax.ShapeDtypeStruct(dims, dtype)


def on_device(
    latents,
    next_latents,
    noise,
    advantage,
    old_logp,
    timesteps,
    embed_weight,
    modulation,
    qkv_weight,
    head_weight,
):
    core = (lax.axis_index("seq") % CORES).reshape(1)
    chip = (lax.axis_index("seq") // CORES).reshape(1)
    rollouts, blocks = lax.axis_size("dp"), lax.axis_size("seq")
    chips = blocks // CORES
    along = [[CORES * (z ^ (chips - 1)) + c for z in range(chips)] for c in range(CORES)]
    latent = latents[0, 0].T
    channels, tokens = latent.shape
    steps_count, _, width = modulation.shape
    rows, columns = qkv_weight.shape[2:]
    wide = CORES * tokens
    head = head_weight[0].T

    def across(value, axis, bits):
        return lax.ppermute(value, axis, [(i, i ^ bits) for i in range(lax.axis_size(axis))])

    steps = call(step_kernel, shape(rollouts, 1, LANES, dtype=jnp.int32), [SMEM], mib=1)(timesteps)
    steps = lax.all_to_all(steps, "dp", 0, 0)[:, 0, 0]
    place = lax.axis_index("dp").reshape(1)
    near, centered, ahead, drawn = call(
        token_kernel,
        [
            shape(channels, tokens, dtype=bf16),
            shape(channels, rows),
            shape(channels, tokens),
            shape(channels, tokens),
        ],
        [SMEM] + [VMEM] * 4,
        flops=10**9,
        mib=16,
    )(place, latent, next_latents[0].T, noise[0].T, embed_weight)

    near = jnp.stack([near, across(near, "seq", 14)])
    near = jnp.concatenate([near] + [across(near, "seq", bits) for bits in (2, 4, 6)], axis=0)
    sums = call(
        partial_kernel,
        shape(steps_count, 6 * channels + 16, LANES, dtype=bf16),
        [SMEM] + [VMEM] * 3,
        [pltpu.VMEM((steps_count * (channels + 16), rows), bf16)],
        flops=3 * 10**9,
        mib=16,
    )(place, centered, modulation, qkv_weight[0])
    sums = call(
        choose_kernel, shape(rollouts, 6 * channels + 16, LANES, dtype=bf16), [SMEM, VMEM], mib=16
    )(steps, sums)

    sums = lax.all_to_all(sums, "dp", 0, 0)
    sums, near = lax.optimization_barrier((sums, near))
    far = across(near, "seq", 1)
    pack, values, offsets = call(
        functools.partial(absorb_kernel, factor=width**-0.5, logit=math.log2(math.e) / HD**0.5),
        [shape(1, 2 * channels + 16, LANES, dtype=bf16), shape(2 * channels, HD), shape(8, HD)],
        [VMEM] * 2,
    )(sums, head)
    pack = jnp.concatenate([pack] + [across(pack, "seq", bits) for bits in (2, 4, 6)], axis=0)
    pack_far = across(pack, "seq", 14)
    keys, spread, own = call(
        tokens_kernel,
        [
            shape(blocks * tokens, LANES, dtype=bf16),
            shape(channels + 16, blocks * tokens, dtype=bf16),
            shape(2 * channels, 2 * wide, dtype=bf16),
        ],
        [SMEM, VMEM, VMEM],
        flops=10**9,
    )(core, near, far)
    def attend(pack, before):
        count = pack.shape[0]
        return call(
            attend_kernel,
            [shape(channels, wide), shape(2 * count, channels, wide, dtype=bf16)],
            [VMEM] * 5,
            [
                pltpu.VMEM((channels, count * LANES), bf16),
                pltpu.VMEM((2 * count, LANES, wide), bf16),
                pltpu.VMEM((2, blocks * tokens, wide), f32),
                pltpu.VMEM((2, 8, wide), f32),
            ],
            flops=4 * 10**9,
        )(pack, keys, spread, own, before)

    shared, attended = attend(pack, jnp.zeros((channels, wide), f32))
    shared, attended_far = attend(pack_far, shared)
    shared = jnp.concatenate([shared, ahead], axis=1)
    other = across(shared, "seq", 1)
    fresh, pieces = call(
        functools.partial(finish_kernel, steps_count=steps_count),
        [shape(channels, tokens, dtype=bf16), shape(chips, channels + 16, LANES, dtype=bf16)],
        [SMEM, SMEM] + [VMEM] * 5,
    )(core, chip, shared, other, attended, attended_far, drawn)
    pieces = lax.all_to_all(pieces, "seq", 0, 0, axis_index_groups=along)
    parts = call(
        functools.partial(gradient_kernel, entries=tokens * blocks * channels),
        shape(rollouts, channels, columns, dtype=bf16),
        [VMEM, VMEM, VMEM, SMEM, SMEM],
    )(pieces, values, offsets, advantage, old_logp)
    parts = lax.all_to_all(parts, "dp", 0, 0, axis_index_groups=[list(reversed(range(rollouts)))])
    gradient, squares = call(
        total_kernel,
        [shape(channels, columns), shape(blocks, 1, LANES)],
        [VMEM],
    )(parts)
    squares = lax.all_to_all(squares, "seq", 0, 0, axis_index_groups=[[(i + blocks // 2) % blocks for i in range(blocks)]])
    role = lax.axis_index("role").reshape(1)
    mine = call(
        functools.partial(update_kernel, entries=columns * blocks * channels),
        shape(channels, columns, dtype=bf16),
        [SMEM] + [VMEM] * 4,
    )(role, gradient, squares, head, fresh)
    other = lax.ppermute(mine, "role", [(0, 1), (1, 0)])
    fresh_out, head_out = call(
        output_kernel,
        [shape(channels, tokens, dtype=bf16), shape(channels, columns, dtype=bf16)],
        [SMEM, VMEM, VMEM],
    )(role, mine, other)
    return (fresh_out.T[None, None], head_out.T[None])


def solution(mesh):
    in_specs = (
        P("role", "dp", "seq", None),
        P("dp", "seq", None),
        P("dp", "seq", None),
        P("dp"),
        P("dp"),
        P("role", "dp"),
        P(),
        P(),
        P("role", None, "dp", "seq"),
        P("role", "seq", None),
    )
    out_specs = (P("role", "dp", "seq", None), P("role", "seq", None))
    return jax.shard_map(
        on_device, mesh=mesh, in_specs=in_specs, out_specs=out_specs, check_vma=False
    )
```
